256 devices in a mesh: ctx: 64 (over z, x_hi, y), head: 4 (over x_lo, core).
Axes of the slice: x: 4 (x_hi: 2, x_lo: 2; x = x_hi * 2 + x_lo), y: 4, z: 8, core: 2. Of those that a mesh axis runs over, the one named last changes fastest.
Arguments:
- query: bfloat16 [32768, 4096], P(('ctx', 'head')), may hold values from -16 to 16
- key: bfloat16 [32768, 4096], P(('ctx', 'head')), may hold values from -4.5 to 4.5
- value: bfloat16 [32768, 4096], P(('ctx', 'head')), may hold values from -12 to 12
- out_grad: bfloat16 [32768, 4096], P(('ctx', 'head')), may hold values from -6 to 6
- offsets: int32 [2, 32], P(None, 'head'), may hold values from 0 to 63, as said below
Outputs:
- attended: bfloat16 [32768, 4096], P(('ctx', 'head'))
- query_grad: bfloat16 [32768, 4096], P(('ctx', 'head'))
- key_grad: bfloat16 [32768, 4096], P(('ctx', 'head'))
- value_grad: bfloat16 [32768, 4096], P(('ctx', 'head'))
The draws below stay inside these ranges and needn't reach their ends.
Inputs may be any that keep to these rules, and one draw needn't show every extreme that they name: `offsets`: row 0 holds values 0 to 15 with 15 among them; row 1 holds values 0 to 63 with 63 among them.
All inputs are finite; a program needn't handle non-finite values.
Results may differ from the reference program's by a relative error of at most 0.04.
Values may be sent and summed in bfloat16 or wider, within the bound.
No kernel may reach another device: no remote copies, remote signals or barrier semaphores. Data moves between devices by JAX's collectives and lax.ppermute only.
A program may use at most 128 MiB of HBM per device.

```python
import jax
import jax.numpy as jnp
from jax import lax

HEADS = 32
HEAD_WIDTH = 128
TOKENS_PER_SLOT = 512
MIDDLE_DILATION = 16
UPPER_DILATION = 64
WIDTH = 4096
TOKEN_COUNT = 32768


def draw_key(key, part):
    key = jax.random.fold_in(key, 3)
    values = jnp.clip(jax.random.normal(key, (TOKEN_COUNT, HEADS * HEAD_WIDTH), jnp.float32), -4.0, 4.0)
    return values.astype(jnp.bfloat16)


def draw_query(key, part):
    key = jax.random.fold_in(key, 5)
    values = jnp.clip(jax.random.normal(jax.random.fold_in(key, 2), (TOKEN_COUNT, HEADS * HEAD_WIDTH), jnp.float32), -4.0, 4.0)
    return values.astype(jnp.bfloat16)


def draw_offsets(key, part):
    key = jax.random.fold_in(key, 11)
    raw = jax.random.randint(key, (2, HEADS), 0, 1 << 20)
    dilation_rates = jnp.array([MIDDLE_DILATION, UPPER_DILATION], jnp.int32)[:, None]
    values = raw % dilation_rates
    chosen = jax.random.randint(jax.random.fold_in(key, 1), (2, 1), 0, HEADS)
    columns = lax.broadcasted_iota(jnp.int32, (2, HEADS), 1)
    return jnp.where(columns == chosen, dilation_rates - 1, values).astype(jnp.int32)


def shard_levels(key, dims, cuts, low, high):
    loudness = 1.0
    for position, blocks in cuts:
        draws = jax.random.uniform(jax.random.fold_in(jax.random.fold_in(key, 6), position), (blocks,), jnp.float32, low / len(cuts), high / len(cuts))
        loudness = loudness * jnp.repeat(jnp.exp(draws), dims[position] // blocks).reshape((-1,) + (1,) * (len(dims) - 1 - position))
    return loudness


def gaussian(key, shape, width, most, cuts=(), held_as=jnp.bfloat16):
    entries = jax.random.normal(key, shape, jnp.float32) * width
    if len(cuts) > 0:
        entries = shard_levels(key, shape, cuts, -0.22, 0.18) * entries
    return jnp.clip(entries, min=-most, max=most).astype(held_as)


def setup_inputs(seed: int = 0) -> dict:
    key_list = jax.random.split(jax.random.key(seed), 6)
    query = draw_query(jax.random.fold_in(key_list[5], 71), 0)
    key = draw_key(jax.random.fold_in(key_list[5], 71), 0)
    value = gaussian(key_list[2], (TOKEN_COUNT, WIDTH), 3.0, 12.0, ((0, 256),))
    out_grad = gaussian(key_list[3], (TOKEN_COUNT, WIDTH), 1.0, 6.0, ((0, 256),))
    offsets = draw_offsets(jax.random.fold_in(key_list[5], 71), 0)
    return {"query": query, "key": key, "value": value, "out_grad": out_grad, "offsets": offsets}


def rounded_length(values):
    return lax.optimization_barrier(values.astype(jnp.bfloat16)).astype(jnp.float32)


def pick_rows(values, dilation_rate, start_offset):
    shaped = values.reshape((values.shape[0] // dilation_rate, dilation_rate) + values.shape[1:])
    return lax.dynamic_index_in_dim(shaped, start_offset, 1, keepdims=False)


def scatter_rows(full, rows, dilation_rate, start_offset, combine):
    shaped = full.reshape((full.shape[0] // dilation_rate, dilation_rate) + full.shape[1:])
    column = lax.dynamic_index_in_dim(shaped, start_offset, 1, keepdims=False)
    shaped = lax.dynamic_update_index_in_dim(shaped, combine(column, rows), start_offset, 1)
    return shaped.reshape(full.shape)


def one_head(items):
    query, key, value, grad, middle_offset, upper_offset = items
    softmax_scale = HEAD_WIDTH ** -0.5
    zero_offset = jnp.zeros((), jnp.int32)
    level_specifications = [(1, zero_offset, TOKEN_COUNT // TOKENS_PER_SLOT), (MIDDLE_DILATION, middle_offset.astype(jnp.int32), 4), (UPPER_DILATION, upper_offset.astype(jnp.int32), 1)]
    levels = []
    for dilation_rate, start_offset, segs in level_specifications:
        query_rows_local = pick_rows(query, dilation_rate, start_offset).reshape(segs, -1, HEAD_WIDTH).astype(jnp.float32)
        key_rows_local = pick_rows(key, dilation_rate, start_offset).reshape(segs, -1, HEAD_WIDTH).astype(jnp.float32)
        value_rows_local = pick_rows(value, dilation_rate, start_offset).reshape(segs, -1, HEAD_WIDTH).astype(jnp.float32)
        gradient_rows = pick_rows(grad, dilation_rate, start_offset).reshape(segs, -1, HEAD_WIDTH).astype(jnp.float32)
        logit_score = jnp.einsum('lrz,laz->lra', query_rows_local, key_rows_local) * softmax_scale
        levels.append((dilation_rate, start_offset, segs, query_rows_local, key_rows_local, value_rows_local, gradient_rows, logit_score))
    top = jnp.full((TOKEN_COUNT,), -jnp.inf, jnp.float32)
    for dilation_rate, start_offset, segs, query_rows_local, key_rows_local, value_rows_local, gradient_rows, logit_score in levels:
        top = scatter_rows(top, logit_score.max(-1).reshape(-1), dilation_rate, start_offset, jnp.maximum)
    total = jnp.zeros((TOKEN_COUNT,), jnp.float32)
    numer = jnp.zeros((TOKEN_COUNT, HEAD_WIDTH), jnp.float32)
    for dilation_rate, start_offset, segs, query_rows_local, key_rows_local, value_rows_local, gradient_rows, logit_score in levels:
        shift = pick_rows(top, dilation_rate, start_offset).reshape(segs, -1)
        level_weight = jnp.exp(logit_score - shift[..., None])
        total = scatter_rows(total, level_weight.sum(-1).reshape(-1), dilation_rate, start_offset, jnp.add)
        part = jnp.einsum('rtg,rgi->rti', rounded_length(level_weight), value_rows_local).reshape(-1, HEAD_WIDTH)
        numer = scatter_rows(numer, part, dilation_rate, start_offset, jnp.add)
    attended = (numer / total[:, None]).astype(jnp.bfloat16)
    lse = top + jnp.log(total)
    delta = jnp.sum(grad.astype(jnp.float32) * attended.astype(jnp.float32), -1)
    query_gradient = jnp.zeros((TOKEN_COUNT, HEAD_WIDTH), jnp.float32)
    key_gradient = jnp.zeros((TOKEN_COUNT, HEAD_WIDTH), jnp.float32)
    value_gradient = jnp.zeros((TOKEN_COUNT, HEAD_WIDTH), jnp.float32)
    for dilation_rate, start_offset, segs, query_rows_local, key_rows_local, value_rows_local, gradient_rows, logit_score in levels:
        lse_rows = pick_rows(lse, dilation_rate, start_offset).reshape(segs, -1)
        delta_rows = pick_rows(delta, dilation_rate, start_offset).reshape(segs, -1)
        probability = jnp.exp(logit_score - lse_rows[..., None])
        probability_gradient = jnp.einsum('lrz,laz->lra', gradient_rows, value_rows_local)
        score_gradient = rounded_length(probability * (probability_gradient - delta_rows[..., None]))
        query_gradient = scatter_rows(query_gradient, (softmax_scale * jnp.einsum('rtg,rgi->rti', score_gradient, key_rows_local)).reshape(-1, HEAD_WIDTH), dilation_rate, start_offset, jnp.add)
        key_gradient = scatter_rows(key_gradient, (softmax_scale * jnp.einsum('nry,nrz->nyz', score_gradient, query_rows_local)).reshape(-1, HEAD_WIDTH), dilation_rate, start_offset, jnp.add)
        value_gradient = scatter_rows(value_gradient, jnp.einsum('nry,nrz->nyz', rounded_length(probability), gradient_rows).reshape(-1, HEAD_WIDTH), dilation_rate, start_offset, jnp.add)
    return attended, query_gradient.astype(jnp.bfloat16), key_gradient.astype(jnp.bfloat16), value_gradient.astype(jnp.bfloat16)


def reference(query, key, value, out_grad, offsets):
    def heads_first(values):
        return values.reshape(TOKEN_COUNT, HEADS, HEAD_WIDTH).transpose(1, 0, 2)

    def tokens_first(values):
        return values.transpose(1, 0, 2).reshape(TOKEN_COUNT, HEADS * HEAD_WIDTH)

    results = lax.map(one_head, (heads_first(query), heads_first(key), heads_first(value), heads_first(out_grad), offsets[0], offsets[1]))
    return (tokens_first(results[0]), tokens_first(results[1]), tokens_first(results[2]), tokens_first(results[3]))
```

```python
import functools

import jax
import jax.numpy as jnp
from jax import lax
from jax.experimental import pallas as pl
from jax.experimental.pallas import tpu as pltpu
from jax.sharding import PartitionSpec as P

AXES = ("ctx", "head")
SCALE = 128.0 ** -0.5
F32 = jnp.float32
BF16 = jnp.bfloat16
VMEM_LIMIT = 48 * 1024 * 1024


def decode(i):
    return i // 64, i // 32 % 2, i // 16 % 2, i // 4 % 4, i // 2 % 2, i % 2


def encode(s, zl, xh, y, xl, c):
    return ((((s * 2 + zl) * 2 + xh) * 4 + y) * 2 + xl) * 2 + c


def route(move):
    return [(i, encode(*move(*decode(i)))) for i in range(256)]


def rel_route(r):
    return route(lambda s, zl, xh, y, xl, c: (s, zl, xh, y, xl ^ (r >> 1), c ^ (r & 1)))


ZL_ROUTE = route(lambda s, zl, xh, y, xl, c: (s, zl ^ 1, xh, y, xl, c))


def s_route(k):
    return route(lambda s, zl, xh, y, xl, c: ((s + k) % 4, zl, xh, y, xl, c))


def unit_groups():
    groups = {}
    for i in range(256):
        s, zl, xh, y, xl, c = decode(i)
        groups.setdefault((s, zl, xl ^ xh, c), []).append(i)
    return list(groups.values())


def send(value, where):
    return lax.ppermute(value, AXES, where)


def unit_exchange(value):
    return lax.all_to_all(value, AXES, 0, 0, tiled=True, axis_index_groups=unit_groups())


def dot_nt(a, b):
    return lax.dot_general(a, b, (((1,), (1,)), ((), ())), preferred_element_type=F32)


def dot_nn(a, b):
    return lax.dot_general(a, b, (((1,), (0,)), ((), ())), preferred_element_type=F32)


def dot_tn(a, b):
    return lax.dot_general(a, b, (((0,), (0,)), ((), ())), preferred_element_type=F32)


def params():
    return pltpu.CompilerParams(vmem_limit_bytes=VMEM_LIMIT)


def cost(flops, bytes_accessed, exps=0):
    return pl.CostEstimate(flops=flops, bytes_accessed=bytes_accessed, transcendentals=exps)


SMEM = pl.BlockSpec(memory_space=pltpu.SMEM)
VMEM = pl.BlockSpec(memory_space=pltpu.VMEM)
ANY = pl.BlockSpec(memory_space=pl.ANY)


def columns(group, index):
    return pl.ds(pl.multiple_of(group * 1024 + index * 128, 128), 128)


def pack_kernel(meta, first, second, *refs):
    outs, sem = refs[:-1], refs[-1]
    group = meta[64]
    parts = len(outs) // 4
    wide = 1024 // parts
    copies = []
    for part in range(parts):
        for r in range(4):
            at = pl.ds(pl.multiple_of((group ^ r) * 1024 + part * wide, 128), wide)
            out = outs[part * 4 + r]
            for half, source in enumerate((first, second)):
                copies.append(
                    pltpu.make_async_copy(
                        source.at[:, at],
                        out.at[pl.ds(half * 128, 128), :],
                        sem.at[len(copies)],
                    )
                )
    for copy in copies:
        copy.start()
    for copy in copies:
        copy.wait()


def pack(meta, first, second, parts):
    shape = jax.ShapeDtypeStruct((256, 1024 // parts), BF16)
    return pl.pallas_call(
        pack_kernel,
        out_shape=[shape] * (4 * parts),
        in_specs=[SMEM, ANY, ANY],
        out_specs=[ANY] * (4 * parts),
        scratch_shapes=[pltpu.SemaphoreType.DMA((8 * parts,))],
        compiler_params=params(),
        cost_estimate=cost(0, 4 << 20),
        name="pack",
    )(meta, first, second)


def select_kernel(meta, key, value, query, grad, *refs):
    outs, full, tops = refs[:4], refs[4], refs[5]
    group = meta[64]
    for r in range(4):
        for h in range(8):
            head = (group ^ r) * 8 + h
            at = columns(group ^ r, h)
            rows = []
            for a, ref in enumerate((key, value, query, grad)):
                full[a] = ref[:, at].astype(F32)
                rows.append(full[a, pl.ds(meta[head], 8, stride=16), :])
                tops[pl.ds(2 * a, 2), :] = full[a, pl.ds(meta[32 + head], 2, stride=64), :]
            rows.append(tops[...])
            outs[r][:, h * 128 : h * 128 + 128] = jnp.concatenate(rows, 0).astype(BF16)


def select(meta, key, value, query, grad):
    return pl.pallas_call(
        select_kernel,
        out_shape=[jax.ShapeDtypeStruct((40, 1024), BF16)] * 4,
        in_specs=[SMEM] + [VMEM] * 4,
        out_specs=[VMEM] * 4,
        scratch_shapes=[pltpu.VMEM((4, 128, 128), F32), pltpu.VMEM((8, 128), F32)],
        compiler_params=params(),
        cost_estimate=cost(0, 5 << 20),
        name="select",
    )(meta, key, value, query, grad)


def lane(shape):
    return lax.broadcasted_iota(jnp.int32, shape, 1)


def row(shape):
    return lax.broadcasted_iota(jnp.int32, shape, 0)


def softmax_stats(score, dprob):
    top = jnp.max(score, -1, keepdims=True)
    weight = jnp.exp(score - top)
    total = jnp.sum(weight, -1, keepdims=True)
    delta = jnp.sum(weight * dprob, -1, keepdims=True) / total
    return top + jnp.log(total), delta


def stats_kernel(act, kv0, kv1, kv2, kv3, out):
    kvs = (kv0, kv1, kv2, kv3)
    key = jnp.concatenate([kv[:128] for kv in kvs], 0)
    value = jnp.concatenate([kv[128:] for kv in kvs], 0)
    score = dot_nt(act[2], key) * SCALE
    lse, delta = softmax_stats(score, dot_nt(act[3], value))
    at = lane((40, 128))
    out[0] = jnp.where(at == 0, lse, jnp.where(at == 1, delta, 0.0))


def stats(act, kvs):
    return pl.pallas_call(
        stats_kernel,
        grid=(8,),
        out_shape=jax.ShapeDtypeStruct((8, 40, 128), F32),
        in_specs=[pl.BlockSpec((4, 40, 128), lambda h: (0, 0, h))]
        + [pl.BlockSpec((256, 128), lambda h: (0, h))] * 4,
        out_specs=pl.BlockSpec((1, 40, 128), lambda h: (h, 0, 0)),
        compiler_params=params(),
        cost_estimate=cost(8 * 40 * 512 * 512, 3 << 20, 8 * 40 * 512),
        name="stats",
    )(act, *kvs)


def split_three(x):
    high = x.astype(BF16)
    rest = x - high.astype(F32)
    middle = rest.astype(BF16)
    low = (rest - middle.astype(F32)).astype(BF16)
    return high.astype(F32), middle.astype(F32), low.astype(F32)


def encode_stats(lse, delta, rows):
    at = lane((rows, 128))
    out = jnp.zeros((rows, 128), F32)
    for index, part in enumerate(split_three(lse) + split_three(delta)):
        out = jnp.where(at == index, part, out)
    return out.astype(BF16)


def decode_stats(x):
    at = lane(x.shape)
    lse = jnp.sum(jnp.where(at < 3, x, 0.0), -1, keepdims=True)
    delta = jnp.sum(jnp.where((at >= 3) & (at < 6), x, 0.0), -1, keepdims=True)
    return lse, delta


def merge_stats(entries):
    top = functools.reduce(jnp.maximum, [lse for lse, _ in entries])
    weights = [jnp.exp(lse - top) for lse, _ in entries]
    total = sum(weights)
    delta = sum(w * d for w, (_, d) in zip(weights, entries)) / total
    return top + jnp.log(total), delta


NONE = -1e30


def unit_kernel(meta, mid, top, oth, t1, t2, t3, st_mid, st_top, out_mid, out_top, mid_oth, top_far):
    head = meta[65]
    o1, o2 = meta[head], meta[32 + head]
    lap = lax.rem(o2, 16) == o1
    shift = lax.div(o2, 16)
    far = (t1, t2, t3)

    def keys(a):
        low = jnp.concatenate([mid[a], oth[a, :256]], 0)
        high = jnp.concatenate([top[a], oth[a, 256:]] + [t[a] for t in far], 0)
        return low, high

    (k1, k2), (v1, v2) = keys(0), keys(1)
    q1, g1, q2, g2 = mid[2], mid[3], top[2], top[3]
    s1, s2 = dot_nt(q1, k1) * SCALE, dot_nt(q2, k2) * SCALE
    p1, p2 = dot_nt(g1, v1), dot_nt(g2, v2)
    lse1, d1 = softmax_stats(s1, p1)
    lse2, d2 = softmax_stats(s2, p2)
    up = (lane((64, 256)) == 4 * row((64, 256)) + shift) & lap
    down = (row((256, 64)) == 4 * lane((256, 64)) + shift) & lap
    one = jnp.ones((), F32)
    none = jnp.zeros((), F32)
    at_top = dot_nn(jnp.where(up, one, none).astype(BF16), encode_stats(lse1, d1, 256))
    at_mid = dot_nn(jnp.where(down, one, none).astype(BF16), encode_stats(lse2, d2, 64))
    lse1_top, d1_top = decode_stats(at_top)
    lse2_mid, d2_mid = decode_stats(at_mid)
    lse1_top = jnp.where(lap, lse1_top, NONE)
    has = (lax.rem(row((256, 1)), 4) == shift) & lap
    lse2_mid = jnp.where(has, lse2_mid, NONE)

    def pick(st):
        at = lane(st.shape)
        return (
            jnp.sum(jnp.where(at == 0, st, 0.0), -1, keepdims=True),
            jnp.sum(jnp.where(at == 1, st, 0.0), -1, keepdims=True),
        )

    lse_m, delta_m = merge_stats([pick(st_mid[...]), (lse1, d1), (lse2_mid, d2_mid)])
    lse_t, delta_t = merge_stats([pick(st_top[...]), (lse2, d2), (lse1_top, d1_top)])

    def back(score, dprob, lse, delta, q, k, v, g):
        prob = jnp.exp(score - lse)
        dscore = (prob * (dprob - delta)).astype(BF16)
        prob = prob.astype(BF16)
        return (
            dot_nn(prob, v).astype(BF16),
            (dot_nn(dscore, k) * SCALE).astype(BF16),
            dot_tn(dscore, q) * SCALE,
            dot_tn(prob, g),
        )

    oo, qq, kk, vv = back(s1, p1, lse_m, delta_m, q1, k1, v1, g1)
    out_mid[0] = oo
    out_mid[1] = qq
    out_mid[2] = kk[:256].astype(BF16)
    out_mid[3] = vv[:256].astype(BF16)
    out_mid[4] = encode_stats(lse_m, delta_m, 256)
    mid_oth[0] = kk[256:].astype(BF16)
    mid_oth[1] = vv[256:].astype(BF16)
    oo, qq, kk, vv = back(s2, p2, lse_t, delta_t, q2, k2, v2, g2)
    out_top[0] = oo
    out_top[1] = qq
    out_top[2] = encode_stats(lse_t, delta_t, 64)
    for k in range(4):
        top_far[k, 0] = kk[128 * k : 128 * k + 128].astype(BF16)
        top_far[k, 1] = vv[128 * k : 128 * k + 128].astype(BF16)


def unit(meta, *arrays):
    return pl.pallas_call(
        unit_kernel,
        out_shape=[
            jax.ShapeDtypeStruct((5, 256, 128), BF16),
            jax.ShapeDtypeStruct((3, 64, 128), BF16),
            jax.ShapeDtypeStruct((2, 256, 128), BF16),
            jax.ShapeDtypeStruct((4, 2, 128, 128), BF16),
        ],
        in_specs=[SMEM] + [VMEM] * 8,
        out_specs=[VMEM] * 4,
        compiler_params=params(),
        cost_estimate=cost(6 * 320 * 512 * 256, 2 << 20, 2 * 320 * 512),
        name="unit",
    )(meta, *arrays)


def main_kernel(first, meta, *refs):
    kvs, qgs, oqs = refs[:4], refs[4:8], refs[8:12]
    dk, dv = refs[12:14]
    ds_all, p_all = refs[14:]
    head = meta[64] * 8 + first + pl.program_id(0)
    o1, o2 = meta[head], meta[32 + head]
    key = jnp.concatenate([kv[:128] for kv in kvs], 0)
    value = jnp.concatenate([kv[128:] for kv in kvs], 0)
    for r in range(4):
        query, grad = qgs[r][:128], qgs[r][128:]
        score = dot_nt(query, key) * SCALE
        weight = jnp.exp(score - jnp.max(score, -1, keepdims=True))
        inverse = 1.0 / jnp.sum(weight, -1, keepdims=True)
        attended = (dot_nn(weight.astype(BF16), value) * inverse).astype(BF16)
        delta = jnp.sum(attended.astype(F32) * grad.astype(F32), -1, keepdims=True)
        prob = weight * inverse
        dscore = (prob * (dot_nt(grad, value) - delta)).astype(BF16)
        oqs[r][:128] = attended
        oqs[r][128:] = (dot_nn(dscore, key) * SCALE).astype(BF16)
        ds_all[128 * r : 128 * r + 128] = dscore
        p_all[128 * r : 128 * r + 128] = prob.astype(BF16)
    at = row((128, 128))
    active = (lax.rem(at, 16) == o1) | (lax.rem(at, 64) == o2)

    def rest(half):
        blocks = []
        for r in range(4):
            block = qgs[r][half * 128 : half * 128 + 128].astype(F32)
            blocks.append(jnp.where(active, 0.0, block).astype(BF16))
        return jnp.concatenate(blocks, 0)

    dk[0] = dot_tn(ds_all[...], rest(0)) * SCALE
    dv[0] = dot_tn(p_all[...], rest(1))


def main(meta, kvs, qgs, first, count):
    return pl.pallas_call(
        functools.partial(main_kernel, first),
        grid=(count,),
        out_shape=[jax.ShapeDtypeStruct((256, 128 * count), BF16)] * 4
        + [jax.ShapeDtypeStruct((count, 512, 128), F32)] * 2,
        in_specs=[SMEM]
        + [pl.BlockSpec((256, 128), lambda h: (0, first + h))] * 4
        + [pl.BlockSpec((256, 128), lambda h: (0, h))] * 4,
        out_specs=[pl.BlockSpec((256, 128), lambda h: (0, h))] * 4
        + [pl.BlockSpec((1, 512, 128), lambda h: (h, 0, 0))] * 2,
        scratch_shapes=[pltpu.VMEM((512, 512), BF16)] * 2,
        compiler_params=params(),
        cost_estimate=cost(count * 12 * 512 * 512 * 128 * 2, count << 20, count * 512 * 512),
        name="main",
    )(meta, *kvs, *qgs)


def late_kernel(first, meta, *refs):
    act, back, dk0, dv0 = refs[:4]
    kvs = refs[4:8]
    dkvs, oas = refs[8:12], refs[12:16]
    full = refs[16]
    head = meta[64] * 8 + first + pl.program_id(0)
    o1, o2 = meta[head], meta[32 + head]
    lap = lax.rem(o2, 16) == o1
    shift = lax.div(o2, 16)
    key = jnp.concatenate([kv[:128] for kv in kvs], 0)
    value = jnp.concatenate([kv[128:] for kv in kvs], 0)
    query, grad = act[2], act[3]
    ret = back[0].astype(F32)
    lse, delta = decode_stats(ret[160:200])
    prob = jnp.exp(dot_nt(query, key) * SCALE - lse)
    dscore = (prob * (dot_nt(grad, value) - delta)).astype(BF16)
    prob = prob.astype(BF16)
    o_act, q_act = dot_nn(prob, value), dot_nn(dscore, key) * SCALE
    up = (lane((8, 32)) == 4 * row((8, 32)) + shift) & lap
    up = jnp.where(up, 1.0, 0.0).astype(BF16)
    o_mid = o_act[:32] + ret[0:32]
    q_mid = q_act[:32] + ret[32:64]
    o_top = o_act[32:] + ret[128:136] + dot_nn(up, ret[0:32].astype(BF16))
    q_top = q_act[32:] + ret[136:144] + dot_nn(up, ret[32:64].astype(BF16))
    for r in range(4):
        oas[r][...] = jnp.concatenate(
            [o_mid[8 * r : 8 * r + 8], q_mid[8 * r : 8 * r + 8], o_top, q_top], 0
        ).astype(BF16)
    twice = (row((40, 128)) >= 32) & lap
    for half, (start, weights, rows, mid_at, top_at, scale) in enumerate(
        ((dk0, dscore, query, 64, 144, SCALE), (dv0, prob, grad, 96, 152, 1.0))
    ):
        rows = jnp.where(twice, 0.0, rows.astype(F32)).astype(BF16)
        full[...] = start[0] + dot_tn(weights, rows) * scale
        at_mid = pl.ds(o1, 32, stride=16)
        full[at_mid, :] = full[at_mid, :] + ret[mid_at : mid_at + 32]
        at_top = pl.ds(o2, 8, stride=64)
        full[at_top, :] = full[at_top, :] + ret[top_at : top_at + 8]
        for r in range(4):
            dkvs[r][half * 128 : half * 128 + 128] = full[128 * r : 128 * r + 128].astype(BF16)


def late(meta, act, back, dk0, dv0, kvs, first, count):
    return pl.pallas_call(
        functools.partial(late_kernel, first),
        grid=(count,),
        out_shape=[jax.ShapeDtypeStruct((256, 128 * count), BF16)] * 4
        + [jax.ShapeDtypeStruct((32, 128 * count), BF16)] * 4,
        in_specs=[
            SMEM,
            pl.BlockSpec((4, 40, 128), lambda h: (0, 0, first + h)),
            pl.BlockSpec((1, 200, 128), lambda h: (first + h, 0, 0)),
            pl.BlockSpec((1, 512, 128), lambda h: (h, 0, 0)),
            pl.BlockSpec((1, 512, 128), lambda h: (h, 0, 0)),
        ]
        + [pl.BlockSpec((256, 128), lambda h: (0, first + h))] * 4,
        out_specs=[pl.BlockSpec((256, 128), lambda h: (0, h))] * 4
        + [pl.BlockSpec((32, 128), lambda h: (0, h))] * 4,
        scratch_shapes=[pltpu.VMEM((512, 128), F32)],
        compiler_params=params(),
        cost_estimate=cost(count * 12 * 40 * 512 * 128, count << 20, count * 40 * 512),
        name="late",
    )(meta, act, back, dk0, dv0, *kvs)


def finish_oq_kernel(meta, *refs):
    oqs, oas = refs[:8], refs[8:16]
    attended, query_grad, full = refs[16:]
    group = meta[64]
    for r in range(4):
        for h in range(8):
            head = (group ^ r) * 8 + h
            at = columns(group ^ r, h)
            part, near = h // 4, h % 4 * 128
            rows = oas[part * 4 + r][:, near : near + 128].astype(F32)
            for half, out in enumerate((attended, query_grad)):
                block = oqs[part * 4 + r][half * 128 : half * 128 + 128, near : near + 128]
                full[half] = block.astype(F32)
                full[half, pl.ds(meta[head], 8, stride=16), :] = rows[8 * half : 8 * half + 8]
                from_row = 16 + 8 * half + 2 * r
                full[half, pl.ds(meta[32 + head], 2, stride=64), :] = rows[from_row : from_row + 2]
                out[:, at] = full[half].astype(BF16)


def finish_oq(meta, oqs, oas):
    return pl.pallas_call(
        finish_oq_kernel,
        out_shape=[jax.ShapeDtypeStruct((128, 4096), BF16)] * 2,
        in_specs=[SMEM] + [VMEM] * 16,
        out_specs=[VMEM] * 2,
        scratch_shapes=[pltpu.VMEM((2, 128, 128), F32)],
        compiler_params=params(),
        cost_estimate=cost(0, 5 << 20),
        name="finish_oq",
    )(meta, *oqs, *oas)


def finish_kv_kernel(meta, *refs):
    dkvs, key_grad, value_grad, sem = refs[:8], refs[8], refs[9], refs[10]
    group = meta[64]
    copies = []
    for part in range(2):
        for r in range(4):
            at = pl.ds(pl.multiple_of((group ^ r) * 1024 + part * 512, 128), 512)
            for half, out in enumerate((key_grad, value_grad)):
                copies.append(
                    pltpu.make_async_copy(
                        dkvs[part * 4 + r].at[pl.ds(half * 128, 128), :],
                        out.at[:, at],
                        sem.at[len(copies)],
                    )
                )
    for copy in copies:
        copy.start()
    for copy in copies:
        copy.wait()


def finish_kv(meta, dkvs):
    return pl.pallas_call(
        finish_kv_kernel,
        out_shape=[jax.ShapeDtypeStruct((128, 4096), BF16)] * 2,
        in_specs=[SMEM] + [ANY] * 8,
        out_specs=[ANY] * 2,
        scratch_shapes=[pltpu.SemaphoreType.DMA((16,))],
        compiler_params=params(),
        cost_estimate=cost(0, 4 << 20),
        name="finish_kv",
    )(meta, *dkvs)


def local(query, key, value, out_grad, offsets):
    place = lax.axis_index("ctx")
    slot = lax.axis_index("head")
    xh, y = place // 4 % 2, place % 4
    group = slot ^ (2 * xh)
    routes = [None] + [rel_route(r) for r in (1, 2, 3)]

    def spread(blocks):
        return [blocks[0]] + [send(blocks[r], routes[r]) for r in (1, 2, 3)]

    rel = jnp.stack(spread([offsets] * 4))
    rel = jnp.where(slot % 2 == 1, rel[jnp.array([1, 0, 3, 2])], rel)
    rel = jnp.where(slot // 2 == 1, rel[jnp.array([2, 3, 0, 1])], rel)
    table = rel.transpose(1, 0, 2).reshape(64)
    meta = jnp.concatenate([table, jnp.stack([group, group * 8 + xh * 4 + y])])
    place_meta = jnp.concatenate([jnp.zeros((64,), jnp.int32), jnp.stack([group, group])])

    kvs = pack(place_meta, key, value, 1)
    acts = spread(select(meta, key, value, query, out_grad))
    kvs = spread(kvs)
    qgs = pack(place_meta, query, out_grad, 2)
    qgs = [spread(qgs[:4]), spread(qgs[4:])]

    stack = jnp.stack(acts)
    act_mid = stack[:, :32].reshape(4, 4, 8, 1024).transpose(1, 0, 2, 3).reshape(4, 32, 1024)
    act_top = stack[:, 32:].reshape(4, 4, 2, 1024).transpose(1, 0, 2, 3).reshape(4, 8, 1024)
    act = jnp.concatenate([act_mid, act_top], 1)
    sent = act.reshape(160, 8, 128).transpose(1, 0, 2).reshape(8 * 160, 128)
    got = unit_exchange(sent).reshape(8, 4, 40, 128)
    mid = got[:, :, :32].transpose(1, 0, 2, 3).reshape(4, 256, 128)
    top = got[:, :, 32:].transpose(1, 0, 2, 3).reshape(4, 64, 128)
    oth = send(jnp.concatenate([mid[:2], top[:2]], 1), ZL_ROUTE)
    top_pair = jnp.concatenate([top[:2], oth[:, 256:]], 1)
    far = [send(top_pair, s_route(k)) for k in (1, 2, 3)]

    st = unit_exchange(stats(act, kvs).reshape(320, 128)).reshape(8, 40, 128)
    out_mid, out_top, mid_oth, top_far = unit(
        meta,
        mid,
        top,
        oth,
        *far,
        st[:, :32].reshape(256, 128),
        st[:, 32:].reshape(64, 128),
    )
    near = send(mid_oth, ZL_ROUTE)
    tops = [send(top_far[k], s_route(4 - k)) for k in (1, 2, 3)]
    total = sum(t.astype(F32) for t in tops) + top_far[0].astype(F32)
    total_near = send(total[:, 64:].astype(BF16), ZL_ROUTE)
    top_kv = (total[:, :64] + total_near.astype(F32)).astype(BF16)
    mid_kv = (out_mid[2:4].astype(F32) + near.astype(F32)).astype(BF16)

    def by_source(x):
        return x.reshape(x.shape[0], 8, -1, 128).transpose(1, 0, 2, 3).reshape(8, -1, 128)

    back = jnp.concatenate(
        [
            by_source(out_mid[:2]),
            by_source(mid_kv),
            by_source(out_top[:2]),
            by_source(top_kv),
            by_source(out_mid[4:]),
            by_source(out_top[2:]),
        ],
        1,
    )
    back = unit_exchange(back.reshape(1600, 128)).reshape(8, 200, 128)

    oqs, oas, dkvs = [], [], []
    for part in range(2):
        outs = main(meta, kvs, qgs[part], 4 * part, 4)
        oqs += spread(outs[:4])
        ends = late(meta, act, back, outs[4], outs[5], kvs, 4 * part, 4)
        oas += spread(ends[4:])
        dkvs += spread(ends[:4])
    attended, query_grad = finish_oq(meta, oqs, oas)
    key_grad, value_grad = finish_kv(place_meta, dkvs)
    return attended, query_grad, key_grad, value_grad


def solution(mesh):
    rows = P(AXES, None)
    return jax.shard_map(
        local,
        mesh=mesh,
        in_specs=(rows, rows, rows, rows, P(None, "head")),
        out_specs=(rows, rows, rows, rows),
        check_vma=False,
    )
```

```python
import functools

import jax
import jax.numpy as jnp
from jax import lax
from jax.experimental import pallas as pl
from jax.experimental.pallas import tpu as pltpu
from jax.sharding import PartitionSpec as P

AXES = ("ctx", "head")
SCALE = 128.0 ** -0.5
LOG2E = 1.4426950408889634
F32 = jnp.float32
BF16 = jnp.bfloat16
VMEM_LIMIT = 60 * 1024 * 1024


def decode(i):
    return i // 64, i // 32 % 2, i // 16 % 2, i // 4 % 4, i // 2 % 2, i % 2


def encode(s, zl, xh, y, xl, c):
    return ((((s * 2 + zl) * 2 + xh) * 4 + y) * 2 + xl) * 2 + c


def route(move):
    return [(i, encode(*move(*decode(i)))) for i in range(256)]


def rel_route(r):
    return route(lambda s, zl, xh, y, xl, c: (s, zl, xh, y, xl ^ (r >> 1), c ^ (r & 1)))


ZL_ROUTE = route(lambda s, zl, xh, y, xl, c: (s, zl ^ 1, xh, y, xl, c))


def unit_groups():
    groups = {}
    for i in range(256):
        s, zl, xh, y, xl, c = decode(i)
        groups.setdefault((s, zl, xl ^ xh, c), []).append(i)
    return list(groups.values())


def send(value, where):
    return lax.ppermute(value, AXES, where)


def z_groups():
    groups = {}
    for i in range(256):
        groups.setdefault(i % 32, []).append(i)
    return list(groups.values())


def unit_exchange(value, groups):
    flat = value.reshape(value.shape[0] * value.shape[1], 128)
    return lax.all_to_all(flat, AXES, 0, 0, tiled=True, axis_index_groups=groups).reshape(value.shape)


def dot_nt(a, b):
    return lax.dot_general(a, b, (((1,), (1,)), ((), ())), preferred_element_type=F32)


def dot_nn(a, b):
    return lax.dot_general(a, b, (((1,), (0,)), ((), ())), preferred_element_type=F32)


def dot_tn(a, b):
    return lax.dot_general(a, b, (((0,), (0,)), ((), ())), preferred_element_type=F32)


def params():
    return pltpu.CompilerParams(vmem_limit_bytes=VMEM_LIMIT)


COST = pl.CostEstimate(flops=0, bytes_accessed=1024, transcendentals=0)
SMEM = pl.BlockSpec(memory_space=pltpu.SMEM)
VMEM = pl.BlockSpec(memory_space=pltpu.VMEM)
ANY = pl.BlockSpec(memory_space=pl.ANY)


def columns(group, index):
    return pl.ds(pl.multiple_of(group * 1024 + index * 128, 128), 128)


def head_offsets(meta, r, h):
    at = (r ^ meta[65]) * 16 + h
    return meta[at], meta[at + 8]


def open_kernel(meta, key, value, query, grad, *refs):
    acts, blocks = refs[:4], refs[4:12]
    held, full, tops, sems, loads = refs[12:]
    group = meta[64]
    ready = []
    for a, ref in enumerate((key, value, query, grad)):
        ready.append(pltpu.make_async_copy(ref, held.at[a], loads.at[a]))
        ready[a].start()
    copies = []
    for a in range(4):
        ready[a].wait()
        for r in range(4):
            at = pl.ds(pl.multiple_of((group ^ r) * 1024, 128), 1024)
            to = blocks[a // 2 * 4 + r].at[pl.ds(a % 2 * 128, 128), :]
            copies.append(pltpu.make_async_copy(held.at[a, :, at], to, sems.at[4 * a + r]))
            copies[-1].start()
    for r in range(4):
        for h in range(8):
            o1, o2 = head_offsets(meta, r, h)
            at = columns(group ^ r, h)
            rows = []
            for a in range(4):
                full[a] = held[a, :, at].astype(F32)
                rows.append(full[a, pl.ds(o1, 8, stride=16), :])
                tops[pl.ds(2 * a, 2), :] = full[a, pl.ds(o2, 2, stride=64), :]
            rows.append(tops[...])
            acts[r][:, h * 128 : h * 128 + 128] = jnp.concatenate(rows, 0).astype(BF16)
    for copy in copies:
        copy.wait()


def open_blocks(meta, key, value, query, grad):
    outs = pl.pallas_call(
        open_kernel,
        out_shape=[jax.ShapeDtypeStruct((40, 1024), BF16)] * 4
        + [jax.ShapeDtypeStruct((256, 1024), BF16)] * 8,
        in_specs=[SMEM] + [ANY] * 4,
        out_specs=[VMEM] * 4 + [ANY] * 8,
        scratch_shapes=[
            pltpu.VMEM((4, 128, 4096), BF16),
            pltpu.VMEM((4, 128, 128), F32),
            pltpu.VMEM((8, 128), F32),
            pltpu.SemaphoreType.DMA((16,)),
            pltpu.SemaphoreType.DMA((4,)),
        ],
        compiler_params=params(),
        cost_estimate=COST,
        name="open",
    )(meta, key, value, query, grad)
    return outs[:4], outs[4:8], outs[8:]


def arrange_kernel(a0, a1, a2, a3, *refs):
    act, out = refs[3:5]
    mid = [[] for _ in range(4)]
    top = [[] for _ in range(4)]
    for ref in (a0, a1, a2, a3):
        x = ref[...].astype(F32)
        for a in range(4):
            mid[a].append(x[8 * a : 8 * a + 8])
            top[a].append(x[32 + 2 * a : 34 + 2 * a])
    rows = []
    for a in range(4):
        rows.append(jnp.concatenate(mid[a] + [jnp.concatenate(top[a], 0)], 0))
        act[a] = rows[a].astype(BF16)
    whole = jnp.concatenate(rows, 0).astype(BF16)
    for h in range(8):
        out[h] = whole[:, 128 * h : 128 * h + 128]


def arrange(acts, blocks):
    outs = pl.pallas_call(
        arrange_kernel,
        out_shape=[
            jax.ShapeDtypeStruct((4, 40, 1024), BF16),
            jax.ShapeDtypeStruct((8, 160, 128), BF16),
        ]
        + [jax.ShapeDtypeStruct((256, 1024), BF16)] * 3,
        in_specs=[VMEM] * 4 + [ANY] * 3,
        out_specs=[VMEM] * 2 + [ANY] * 3,
        input_output_aliases={4: 2, 5: 3, 6: 4},
        compiler_params=params(),
        cost_estimate=COST,
        name="arrange",
    )(*acts, *blocks)
    return outs[0], outs[1], outs[2:]


def fan_kernel(got, mid, top, far):
    blocks = [got[j].astype(F32) for j in range(8)]
    tops = []
    for a in range(4):
        at = 40 * a
        mid[a] = jnp.concatenate([x[at : at + 32] for x in blocks], 0).astype(BF16)
        tops.append(jnp.concatenate([x[at + 32 : at + 40] for x in blocks], 0))
        top[a] = tops[a].astype(BF16)
    both_rows = jnp.concatenate(tops[:2], 0).astype(BF16)
    for z in range(8):
        far[z] = both_rows


def fan(got):
    return pl.pallas_call(
        fan_kernel,
        out_shape=[
            jax.ShapeDtypeStruct((4, 256, 128), BF16),
            jax.ShapeDtypeStruct((4, 64, 128), BF16),
            jax.ShapeDtypeStruct((8, 128, 128), BF16),
        ],
        in_specs=[VMEM],
        out_specs=[VMEM] * 3,
        compiler_params=params(),
        cost_estimate=COST,
        name="fan",
    )(got)


def lane(shape):
    return lax.broadcasted_iota(jnp.int32, shape, 1)


def row(shape):
    return lax.broadcasted_iota(jnp.int32, shape, 0)


def softmax_stats(score, dprob):
    top = jnp.max(score, -1, keepdims=True)
    weight = jnp.exp(score - top)
    total = jnp.sum(weight, -1, keepdims=True)
    delta = jnp.sum(weight * dprob, -1, keepdims=True) / total
    return top + jnp.log(total), delta


def stats_kernel(act, *refs):
    kvs, out = refs[:4], refs[-1]
    for h in range(8):
        at = pl.ds(128 * h, 128)
        key = jnp.concatenate([kv[:128, at] for kv in kvs], 0)
        value = jnp.concatenate([kv[128:, at] for kv in kvs], 0)
        score = dot_nt(key, act[2, :, at]) * SCALE
        top = jnp.max(score, 0, keepdims=True)
        weight = jnp.exp(score - top)
        total = jnp.sum(weight, 0, keepdims=True)
        dprob = dot_nt(value, act[3, :, at])
        out[h, 0:1, 0:40] = top + jnp.log(total)
        out[h, 1:2, 0:40] = jnp.sum(weight * dprob, 0, keepdims=True) / total


def stats(act, kvs, last):
    return pl.pallas_call(
        stats_kernel,
        out_shape=jax.ShapeDtypeStruct((8, 8, 128), F32),
        in_specs=[VMEM] * 5 + [ANY] * len(last),
        out_specs=VMEM,
        compiler_params=params(),
        cost_estimate=COST,
        name="stats",
    )(act, *kvs, *last)


def split_three(x):
    high = x.astype(BF16)
    rest = x - high.astype(F32)
    middle = rest.astype(BF16)
    low = (rest - middle.astype(F32)).astype(BF16)
    return high.astype(F32), middle.astype(F32), low.astype(F32)


def encode_stats(lse, delta, rows):
    at = lane((rows, 128))
    out = jnp.zeros((rows, 128), F32)
    for index, part in enumerate(split_three(lse) + split_three(delta)):
        out = jnp.where(at == index, part, out)
    return out.astype(BF16)


def decode_stats(x):
    at = lane(x.shape)
    lse = jnp.sum(jnp.where(at < 3, x, 0.0), -1, keepdims=True)
    delta = jnp.sum(jnp.where((at >= 3) & (at < 6), x, 0.0), -1, keepdims=True)
    return lse, delta


def merge_stats(entries):
    top = functools.reduce(jnp.maximum, [lse for lse, _ in entries])
    weights = [jnp.exp(lse - top) for lse, _ in entries]
    total = sum(weights)
    delta = sum(w * d for w, (_, d) in zip(weights, entries)) / total
    return top + jnp.log(total), delta


NONE = -1e30


def unit_kernel(meta, mid, top, oth, topz, st, *refs):
    out_mid, out_top, mid_oth, top_far = refs[-4:]
    o1, o2 = head_offsets(meta, 0, meta[66])
    lap = lax.rem(o2, 16) == o1
    shift = lax.div(o2, 16)
    k1, v1 = (jnp.concatenate([mid[a], oth[a]], 0) for a in range(2))
    k2 = jnp.concatenate([topz[z, :64] for z in range(8)], 0)
    v2 = jnp.concatenate([topz[z, 64:] for z in range(8)], 0)
    q1, g1, q2, g2 = mid[2], mid[3], top[2], top[3]
    level0 = []
    for index in range(2):
        rows = jnp.concatenate([st[j, index : index + 1, :] for j in range(8)], 0).T
        level0.append(
            (
                jnp.concatenate([rows[:32, j : j + 1] for j in range(8)], 0),
                jnp.concatenate([rows[32:40, j : j + 1] for j in range(8)], 0),
            )
        )
    s1, s2 = dot_nt(q1, k1) * SCALE, dot_nt(q2, k2) * SCALE
    p1, p2 = dot_nt(g1, v1), dot_nt(g2, v2)
    lse1, d1 = softmax_stats(s1, p1)
    lse2, d2 = softmax_stats(s2, p2)
    up = (lane((64, 256)) == 4 * row((64, 256)) + shift) & lap
    down = (row((256, 64)) == 4 * lane((256, 64)) + shift) & lap
    one = jnp.ones((), F32)
    none = jnp.zeros((), F32)
    at_top = dot_nn(jnp.where(up, one, none).astype(BF16), encode_stats(lse1, d1, 256))
    at_mid = dot_nn(jnp.where(down, one, none).astype(BF16), encode_stats(lse2, d2, 64))
    lse1_top, d1_top = decode_stats(at_top)
    lse2_mid, d2_mid = decode_stats(at_mid)
    lse1_top = jnp.where(lap, lse1_top, NONE)
    has = (lax.rem(row((256, 1)), 4) == shift) & lap
    lse2_mid = jnp.where(has, lse2_mid, NONE)

    lse_m, delta_m = merge_stats([(level0[0][0], level0[1][0]), (lse1, d1), (lse2_mid, d2_mid)])
    lse_t, delta_t = merge_stats([(level0[0][1], level0[1][1]), (lse2, d2), (lse1_top, d1_top)])

    def back(score, dprob, lse, delta, q, k, v, g):
        prob = jnp.exp(score - lse)
        dscore = (prob * (dprob - delta)).astype(BF16)
        prob = prob.astype(BF16)
        return (
            dot_nn(prob, v).astype(BF16),
            (dot_nn(dscore, k) * SCALE).astype(BF16),
            dot_tn(dscore, q) * SCALE,
            dot_tn(prob, g),
        )

    oo, qq, kk, vv = back(s1, p1, lse_m, delta_m, q1, k1, v1, g1)
    out_mid[0] = oo
    out_mid[1] = qq
    out_mid[2] = kk[:256].astype(BF16)
    out_mid[3] = vv[:256].astype(BF16)
    out_mid[4] = encode_stats(lse_m, delta_m, 256)
    mid_oth[0] = kk[256:].astype(BF16)
    mid_oth[1] = vv[256:].astype(BF16)
    oo, qq, kk, vv = back(s2, p2, lse_t, delta_t, q2, k2, v2, g2)
    out_top[0] = oo
    out_top[1] = qq
    out_top[2] = encode_stats(lse_t, delta_t, 64)
    for z in range(8):
        top_far[z, :64] = kk[64 * z : 64 * z + 64].astype(BF16)
        top_far[z, 64:] = vv[64 * z : 64 * z + 64].astype(BF16)


def unit(meta, arrays, last):
    return pl.pallas_call(
        unit_kernel,
        out_shape=[
            jax.ShapeDtypeStruct((5, 256, 128), BF16),
            jax.ShapeDtypeStruct((3, 64, 128), BF16),
            jax.ShapeDtypeStruct((2, 256, 128), BF16),
            jax.ShapeDtypeStruct((8, 128, 128), BF16),
        ],
        in_specs=[SMEM] + [VMEM] * 5 + [ANY] * len(last),
        out_specs=[VMEM] * 4,
        compiler_params=params(),
        cost_estimate=COST,
        name="unit",
    )(meta, *arrays, *last)


def combine_kernel(out_mid, out_top, near, tops, *refs):
    back = refs[-1]
    top_kv = sum(tops[z].astype(F32) for z in range(8))
    mids = [out_mid[a].astype(F32) for a in range(5)]
    mids[2] = mids[2] + near[0].astype(F32)
    mids[3] = mids[3] + near[1].astype(F32)
    outs = [out_top[a].astype(F32) for a in range(3)]
    highs = [outs[0], outs[1], top_kv[:64], top_kv[64:]]
    for j in range(8):
        rows = [x[32 * j : 32 * j + 32] for x in mids[:4]]
        rows += [x[8 * j : 8 * j + 8] for x in highs]
        rows += [mids[4][32 * j : 32 * j + 32], outs[2][8 * j : 8 * j + 8]]
        back[j] = jnp.concatenate(rows, 0).astype(BF16)


def combine(arrays, last):
    return pl.pallas_call(
        combine_kernel,
        out_shape=jax.ShapeDtypeStruct((8, 200, 128), BF16),
        in_specs=[VMEM] * 4 + [ANY] * len(last),
        out_specs=VMEM,
        compiler_params=params(),
        cost_estimate=COST,
        name="combine",
    )(*arrays, *last)


def main_kernel(first, meta, *refs):
    kvs, qgs = refs[:4], refs[4:8]
    oqs, dk, dv = refs[-6:-2], refs[-2], refs[-1]
    o1, o2 = head_offsets(meta, 0, first + pl.program_id(0))
    key = jnp.concatenate([kv[:128] for kv in kvs], 0)
    value = jnp.concatenate([kv[128:] for kv in kvs], 0)
    query = jnp.concatenate([qg[:128] for qg in qgs], 0)
    grad = jnp.concatenate([qg[128:] for qg in qgs], 0)
    score = dot_nt(key, query) * (SCALE * LOG2E)
    weight = jnp.exp2(score - jnp.max(score, 0, keepdims=True))
    inverse = 1.0 / jnp.sum(weight, 0, keepdims=True)
    attended = dot_nn(value.T, weight.astype(BF16)) * inverse
    delta = jnp.sum(attended * grad.astype(F32).T, 0, keepdims=True)
    prob = weight * inverse
    dscore = (prob * (dot_nt(value, grad) - delta)).astype(BF16)
    attended = attended.T.astype(BF16)
    query_grad = (dot_nn(key.T, dscore) * SCALE).T.astype(BF16)
    for r in range(4):
        oqs[r][:128] = attended[128 * r : 128 * r + 128]
        oqs[r][128:] = query_grad[128 * r : 128 * r + 128]
    at = row((512, 128))
    active = (lax.rem(at, 16) == o1) | (lax.rem(at, 64) == o2)
    zero = jnp.zeros((), BF16)
    dk[0] = dot_nn(dscore, jnp.where(active, zero, query)) * SCALE
    dv[0] = dot_nn(prob.astype(BF16), jnp.where(active, zero, grad))


def head_block(rows, first):
    return pl.BlockSpec((rows, 128), lambda h: (0, first + h))


def part_shapes(rows):
    return [jax.ShapeDtypeStruct((rows, 1024), BF16)] * 2 + [
        jax.ShapeDtypeStruct((rows, 512), BF16)
    ] * 2


def part_specs(rows, first):
    return [head_block(rows, first)] * 2 + [head_block(rows, 0)] * 2


def main(meta, kvs, qgs, first, held, last):
    before = [meta, *kvs, *qgs, *last]
    return pl.pallas_call(
        functools.partial(main_kernel, first),
        grid=(4,),
        out_shape=part_shapes(256) + [jax.ShapeDtypeStruct((4, 512, 128), F32)] * 2,
        in_specs=[SMEM]
        + [head_block(256, first)] * 8
        + [ANY] * (len(last) + len(held)),
        out_specs=part_specs(256, first)
        + [pl.BlockSpec((1, 512, 128), lambda h: (h, 0, 0))] * 2,
        input_output_aliases={len(before) + i: i for i in range(len(held))},
        compiler_params=params(),
        cost_estimate=COST,
        name="main",
    )(*before, *held)


def late_kernel(first, meta, *refs):
    act, back, dk0, dv0 = refs[:4]
    kvs = refs[4:8]
    dkvs, oas, full = refs[-9:-5], refs[-5:-1], refs[-1]
    o1, o2 = head_offsets(meta, 0, first + pl.program_id(0))
    lap = lax.rem(o2, 16) == o1
    shift = lax.div(o2, 16)
    key = jnp.concatenate([kv[:128] for kv in kvs], 0)
    value = jnp.concatenate([kv[128:] for kv in kvs], 0)
    query, grad = act[2], act[3]
    ret = back[0].astype(F32)
    lse, delta = decode_stats(ret[160:200])
    prob = jnp.exp(dot_nt(query, key) * SCALE - lse)
    dscore = (prob * (dot_nt(grad, value) - delta)).astype(BF16)
    prob = prob.astype(BF16)
    o_act, q_act = dot_nn(prob, value), dot_nn(dscore, key) * SCALE
    up = (lane((8, 32)) == 4 * row((8, 32)) + shift) & lap
    up = jnp.where(up, 1.0, 0.0).astype(BF16)
    o_mid = o_act[:32] + ret[0:32]
    q_mid = q_act[:32] + ret[32:64]
    o_top = o_act[32:] + ret[128:136] + dot_nn(up, ret[0:32].astype(BF16))
    q_top = q_act[32:] + ret[136:144] + dot_nn(up, ret[32:64].astype(BF16))
    for r in range(4):
        oas[r][...] = jnp.concatenate(
            [o_mid[8 * r : 8 * r + 8], q_mid[8 * r : 8 * r + 8], o_top, q_top], 0
        ).astype(BF16)
    twice = (row((40, 128)) >= 32) & lap
    for half, (start, weights, rows, mid_at, top_at, scale) in enumerate(
        ((dk0, dscore, query, 64, 144, SCALE), (dv0, prob, grad, 96, 152, 1.0))
    ):
        rows = jnp.where(twice, 0.0, rows.astype(F32)).astype(BF16)
        full[...] = start[0] + dot_tn(weights, rows) * scale
        at_mid = pl.ds(o1, 32, stride=16)
        full[at_mid, :] = full[at_mid, :] + ret[mid_at : mid_at + 32]
        at_top = pl.ds(o2, 8, stride=64)
        full[at_top, :] = full[at_top, :] + ret[top_at : top_at + 8]
        for r in range(4):
            dkvs[r][half * 128 : half * 128 + 128] = full[128 * r : 128 * r + 128].astype(BF16)


def late(meta, act, back, dk0, dv0, kvs, first, held, last):
    before = [meta, act, back, dk0, dv0, *kvs, *last]
    places = (0, 1, 4, 5, 6, 7)[: len(held)]
    return pl.pallas_call(
        functools.partial(late_kernel, first),
        grid=(4,),
        out_shape=part_shapes(256) + [jax.ShapeDtypeStruct((32, 1024), BF16)] * 4,
        in_specs=[
            SMEM,
            pl.BlockSpec((4, 40, 128), lambda h: (0, 0, first + h)),
            pl.BlockSpec((1, 200, 128), lambda h: (first + h, 0, 0)),
            pl.BlockSpec((1, 512, 128), lambda h: (h, 0, 0)),
            pl.BlockSpec((1, 512, 128), lambda h: (h, 0, 0)),
        ]
        + [head_block(256, first)] * 4
        + [ANY] * (len(last) + len(held)),
        out_specs=part_specs(256, first) + [head_block(32, first)] * 4,
        scratch_shapes=[pltpu.VMEM((512, 128), F32)],
        input_output_aliases={len(before) + i: at for i, at in enumerate(places)},
        compiler_params=params(),
        cost_estimate=COST,
        name="late",
    )(*before, *held)


def piece(blocks, r, h):
    if r < 2:
        return blocks[r], 128 * h
    return blocks[2 * (h // 4) + r], h % 4 * 128


def finish_oq_kernel(meta, *refs):
    oqs, oas = refs[:6], refs[6:10]
    attended, query_grad, full = refs[-3:]
    group = meta[64]
    for r in range(4):
        for h in range(8):
            o1, o2 = head_offsets(meta, r, h)
            at = columns(group ^ r, h)
            source, near = piece(oqs, r, h)
            rows = oas[r][:, 128 * h : 128 * h + 128].astype(F32)
            for half, out in enumerate((attended, query_grad)):
                block = source[half * 128 : half * 128 + 128, near : near + 128]
                full[half] = block.astype(F32)
                full[half, pl.ds(o1, 8, stride=16), :] = rows[8 * half : 8 * half + 8]
                from_row = 16 + 8 * half + 2 * r
                full[half, pl.ds(o2, 2, stride=64), :] = rows[from_row : from_row + 2]
                out[:, at] = full[half].astype(BF16)


def finish_oq(meta, oqs, oas, last):
    return pl.pallas_call(
        finish_oq_kernel,
        out_shape=[jax.ShapeDtypeStruct((128, 4096), BF16)] * 2,
        in_specs=[SMEM] + [VMEM] * 10 + [ANY] * len(last),
        out_specs=[VMEM] * 2,
        scratch_shapes=[pltpu.VMEM((2, 128, 128), F32)],
        compiler_params=params(),
        cost_estimate=COST,
        name="finish_oq",
    )(meta, *oqs, *oas, *last)


def finish_kv_kernel(meta, *refs):
    dkvs, outs, held, sems = refs[:6], refs[6:8], refs[8], refs[9]
    group = meta[64]
    copies = []
    for half in range(2):
        for index, block in enumerate(dkvs):
            r = index if index < 4 else index - 2
            wide = 1024 if r < 2 else 512
            start = (group ^ r) * 1024 + (512 if index >= 4 else 0)
            at = pl.ds(pl.multiple_of(start, 128), wide)
            from_rows = block.at[pl.ds(half * 128, 128), :]
            copies.append(
                pltpu.make_async_copy(from_rows, held.at[half, :, at], sems.at[len(copies)])
            )
            copies[-1].start()
    stores = []
    for half in range(2):
        for copy in copies[6 * half : 6 * half + 6]:
            copy.wait()
        stores.append(pltpu.make_async_copy(held.at[half], outs[half], sems.at[12 + half]))
        stores[half].start()
    for copy in stores:
        copy.wait()


def finish_kv(meta, dkvs):
    return pl.pallas_call(
        finish_kv_kernel,
        out_shape=[jax.ShapeDtypeStruct((128, 4096), BF16)] * 2,
        in_specs=[SMEM] + [ANY] * 6,
        out_specs=[ANY] * 2,
        scratch_shapes=[pltpu.VMEM((2, 128, 4096), BF16), pltpu.SemaphoreType.DMA((14,))],
        compiler_params=params(),
        cost_estimate=COST,
        name="finish_kv",
    )(meta, *dkvs)


def local(query, key, value, out_grad, offsets):
    place = lax.axis_index("ctx")
    slot = lax.axis_index("head")
    xh, y = place // 4 % 2, place % 4
    group = slot ^ (2 * xh)
    routes = [None] + [rel_route(r) for r in (1, 2, 3)]
    units, levels = unit_groups(), z_groups()

    def go(block, r):
        return block if r == 0 else send(block, routes[r])

    def spread(blocks):
        return [go(block, r) for r, block in enumerate(blocks)]

    table = jnp.concatenate([block.reshape(16) for block in spread([offsets] * 4)])
    meta = jnp.concatenate([table, jnp.stack([group, 2 * xh, xh * 4 + y])])

    acts, kvs, qgs = open_blocks(meta, key, value, query, out_grad)
    acts = spread(acts)
    act, sent, passed = arrange(acts, kvs[1:])
    kvs = spread([kvs[0], *passed])
    qgs = spread(qgs)

    mid, top, far = fan(unit_exchange(sent, units))
    oth = send(mid[:2], ZL_ROUTE)
    topz = unit_exchange(far, levels)
    st = unit_exchange(stats(act, kvs, [oth, topz]), units)
    out_mid, out_top, mid_oth, top_far = unit(meta, (mid, top, oth, topz, st), [qgs[2]])
    near = send(mid_oth, ZL_ROUTE)
    tops = unit_exchange(top_far, levels)
    first = main(meta, kvs, qgs, 0, [], [top_far])
    second = main(meta, kvs, qgs, 4, first[:2], [])
    oqs = [second[0], go(second[1], 1)]
    oqs += [go(first[2], 2), go(first[3], 3), go(second[2], 2), go(second[3], 3)]
    sums = combine((out_mid, out_top, near, tops), [second[4], oqs[2], oqs[3]])
    back = unit_exchange(sums, units)
    early = late(meta, act, back, first[4], first[5], kvs, 0, [], [oqs[4]])
    dkv2, dkv3 = send(early[2], routes[2]), send(early[3], routes[3])
    held = [early[0], early[1], *early[4:]]
    final = late(meta, act, back, second[4], second[5], kvs, 4, held, [oqs[5]])
    oas = spread(final[4:])
    dkvs = [final[0], go(final[1], 1), dkv2, dkv3, go(final[2], 2), go(final[3], 3)]
    attended, query_grad = finish_oq(meta, oqs, oas, [dkv2])
    key_grad, value_grad = finish_kv(meta, dkvs)
    return attended, query_grad, key_grad, value_grad


def solution(mesh):
    rows = P(AXES, None)
    return jax.shard_map(
        local,
        mesh=mesh,
        in_specs=(rows, rows, rows, rows, P(None, "head")),
        out_specs=(rows, rows, rows, rows),
        check_vma=False,
    )
```

```python
import functools

import jax
import jax.numpy as jnp
from jax import lax
from jax.experimental import pallas as pl
from jax.experimental.pallas import tpu as pltpu
from jax.sharding import PartitionSpec as P

AXES = ("ctx", "head")
SCALE = 128.0 ** -0.5
LOG2E = 1.4426950408889634
F32 = jnp.float32
BF16 = jnp.bfloat16
VMEM_LIMIT = 60 * 1024 * 1024


def decode(i):
    return i // 64, i // 32 % 2, i // 16 % 2, i // 4 % 4, i // 2 % 2, i % 2


def encode(s, zl, xh, y, xl, c):
    return ((((s * 2 + zl) * 2 + xh) * 4 + y) * 2 + xl) * 2 + c


def route(move):
    return [(i, encode(*move(*decode(i)))) for i in range(256)]


def rel_route(r):
    return route(lambda s, zl, xh, y, xl, c: (s, zl, xh, y, xl ^ (r >> 1), c ^ (r & 1)))


ZL_ROUTE = route(lambda s, zl, xh, y, xl, c: (s, zl ^ 1, xh, y, xl, c))


def unit_groups():
    groups = {}
    for i in range(256):
        s, zl, xh, y, xl, c = decode(i)
        groups.setdefault((s, zl, xl ^ xh, c), []).append(i)
    return list(groups.values())


def send(value, where):
    return lax.ppermute(value, AXES, where)


def z_groups():
    groups = {}
    for i in range(256):
        groups.setdefault(i % 32, []).append(i)
    return list(groups.values())


def unit_exchange(value, groups):
    flat = value.reshape(value.shape[0] * value.shape[1], 128)
    return lax.all_to_all(flat, AXES, 0, 0, tiled=True, axis_index_groups=groups).reshape(value.shape)


def dot_nt(a, b):
    return lax.dot_general(a, b, (((1,), (1,)), ((), ())), preferred_element_type=F32)


def dot_nn(a, b):
    return lax.dot_general(a, b, (((1,), (0,)), ((), ())), preferred_element_type=F32)


def dot_tn(a, b):
    return lax.dot_general(a, b, (((0,), (0,)), ((), ())), preferred_element_type=F32)


def params():
    return pltpu.CompilerParams(vmem_limit_bytes=VMEM_LIMIT)


COST = pl.CostEstimate(flops=0, bytes_accessed=1024, transcendentals=0)
SMEM = pl.BlockSpec(memory_space=pltpu.SMEM)
VMEM = pl.BlockSpec(memory_space=pltpu.VMEM)
ANY = pl.BlockSpec(memory_space=pl.ANY)


def columns(group, index):
    return pl.ds(pl.multiple_of(group * 1024 + index * 128, 128), 128)


def head_offsets(meta, r, h):
    at = (r ^ meta[65]) * 16 + h
    return meta[at], meta[at + 8]


def open_kernel(meta, key, value, query, grad, *refs):
    acts, blocks = refs[:4], refs[4:12]
    held, full, tops, sems, loads = refs[12:]
    group = meta[64]
    ready = []
    for a, ref in enumerate((key, value, query, grad)):
        ready.append(pltpu.make_async_copy(ref, held.at[a], loads.at[a]))
        ready[a].start()
    copies = []
    for a in range(4):
        ready[a].wait()
        for r in range(4):
            at = pl.ds(pl.multiple_of((group ^ r) * 1024, 128), 1024)
            to = blocks[a // 2 * 4 + r].at[pl.ds(a % 2 * 128, 128), :]
            copies.append(pltpu.make_async_copy(held.at[a, :, at], to, sems.at[4 * a + r]))
            copies[-1].start()
    for r in range(4):
        for h in range(8):
            o1, o2 = head_offsets(meta, r, h)
            at = columns(group ^ r, h)
            rows = []
            for a in range(4):
                full[a] = held[a, :, at].astype(F32)
                rows.append(full[a, pl.ds(o1, 8, stride=16), :])
                tops[pl.ds(2 * a, 2), :] = full[a, pl.ds(o2, 2, stride=64), :]
            rows.append(tops[...])
            acts[r][:, h * 128 : h * 128 + 128] = jnp.concatenate(rows, 0).astype(BF16)
    for copy in copies:
        copy.wait()


def open_blocks(meta, key, value, query, grad):
    outs = pl.pallas_call(
        open_kernel,
        out_shape=[jax.ShapeDtypeStruct((40, 1024), BF16)] * 4
        + [jax.ShapeDtypeStruct((256, 1024), BF16)] * 8,
        in_specs=[SMEM] + [ANY] * 4,
        out_specs=[VMEM] * 4 + [ANY] * 8,
        scratch_shapes=[
            pltpu.VMEM((4, 128, 4096), BF16),
            pltpu.VMEM((4, 128, 128), F32),
            pltpu.VMEM((8, 128), F32),
            pltpu.SemaphoreType.DMA((16,)),
            pltpu.SemaphoreType.DMA((4,)),
        ],
        compiler_params=params(),
        cost_estimate=COST,
        name="open",
    )(meta, key, value, query, grad)
    return outs[:4], outs[4:8], outs[8:]


def arrange_kernel(a0, a1, a2, a3, *refs):
    act, out = refs[3:5]
    mid = [[] for _ in range(4)]
    top = [[] for _ in range(4)]
    for ref in (a0, a1, a2, a3):
        x = ref[...].astype(F32)
        for a in range(4):
            mid[a].append(x[8 * a : 8 * a + 8])
            top[a].append(x[32 + 2 * a : 34 + 2 * a])
    rows = []
    for a in range(4):
        rows.append(jnp.concatenate(mid[a] + [jnp.concatenate(top[a], 0)], 0))
        act[a] = rows[a].astype(BF16)
    whole = jnp.concatenate(rows, 0).astype(BF16)
    for h in range(8):
        out[h] = whole[:, 128 * h : 128 * h + 128]


def arrange(acts, blocks):
    outs = pl.pallas_call(
        arrange_kernel,
        out_shape=[
            jax.ShapeDtypeStruct((4, 40, 1024), BF16),
            jax.ShapeDtypeStruct((8, 160, 128), BF16),
        ]
        + [jax.ShapeDtypeStruct((256, 1024), BF16)] * 3,
        in_specs=[VMEM] * 4 + [ANY] * 3,
        out_specs=[VMEM] * 2 + [ANY] * 3,
        input_output_aliases={4: 2, 5: 3, 6: 4},
        compiler_params=params(),
        cost_estimate=COST,
        name="arrange",
    )(*acts, *blocks)
    return outs[0], outs[1], outs[2:]


def fan_kernel(got, mid, top, far):
    blocks = [got[j].astype(F32) for j in range(8)]
    tops = []
    for a in range(4):
        at = 40 * a
        mid[a] = jnp.concatenate([x[at : at + 32] for x in blocks], 0).astype(BF16)
        tops.append(jnp.concatenate([x[at + 32 : at + 40] for x in blocks], 0))
        top[a] = tops[a].astype(BF16)
    both_rows = jnp.concatenate(tops[:2], 0).astype(BF16)
    for z in range(8):
        far[z] = both_rows


def fan(got):
    return pl.pallas_call(
        fan_kernel,
        out_shape=[
            jax.ShapeDtypeStruct((4, 256, 128), BF16),
            jax.ShapeDtypeStruct((4, 64, 128), BF16),
            jax.ShapeDtypeStruct((8, 128, 128), BF16),
        ],
        in_specs=[VMEM],
        out_specs=[VMEM] * 3,
        compiler_params=params(),
        cost_estimate=COST,
        name="fan",
    )(got)


def lane(shape):
    return lax.broadcasted_iota(jnp.int32, shape, 1)


def row(shape):
    return lax.broadcasted_iota(jnp.int32, shape, 0)


def softmax_stats(score, dprob):
    top = jnp.max(score, -1, keepdims=True)
    weight = jnp.exp(score - top)
    total = jnp.sum(weight, -1, keepdims=True)
    delta = jnp.sum(weight * dprob, -1, keepdims=True) / total
    return top + jnp.log(total), delta


def stats_kernel(act, *refs):
    kvs, out = refs[:4], refs[-1]
    for h in range(8):
        at = pl.ds(128 * h, 128)
        key = jnp.concatenate([kv[:128, at] for kv in kvs], 0)
        value = jnp.concatenate([kv[128:, at] for kv in kvs], 0)
        score = dot_nt(key, act[2, :, at]) * SCALE
        top = jnp.max(score, 0, keepdims=True)
        weight = jnp.exp(score - top)
        total = jnp.sum(weight, 0, keepdims=True)
        dprob = dot_nt(value, act[3, :, at])
        out[h, 0:1, 0:40] = top + jnp.log(total)
        out[h, 1:2, 0:40] = jnp.sum(weight * dprob, 0, keepdims=True) / total


def stats(act, kvs, last):
    return pl.pallas_call(
        stats_kernel,
        out_shape=jax.ShapeDtypeStruct((8, 8, 128), F32),
        in_specs=[VMEM] * 5 + [ANY] * len(last),
        out_specs=VMEM,
        compiler_params=params(),
        cost_estimate=COST,
        name="stats",
    )(act, *kvs, *last)


def split_three(x):
    high = x.astype(BF16)
    rest = x - high.astype(F32)
    middle = rest.astype(BF16)
    low = (rest - middle.astype(F32)).astype(BF16)
    return high.astype(F32), middle.astype(F32), low.astype(F32)


def encode_stats(lse, delta, rows):
    at = lane((rows, 128))
    out = jnp.zeros((rows, 128), F32)
    for index, part in enumerate(split_three(lse) + split_three(delta)):
        out = jnp.where(at == index, part, out)
    return out.astype(BF16)


def decode_stats(x):
    at = lane(x.shape)
    lse = jnp.sum(jnp.where(at < 3, x, 0.0), -1, keepdims=True)
    delta = jnp.sum(jnp.where((at >= 3) & (at < 6), x, 0.0), -1, keepdims=True)
    return lse, delta


def merge_stats(entries):
    top = functools.reduce(jnp.maximum, [lse for lse, _ in entries])
    weights = [jnp.exp(lse - top) for lse, _ in entries]
    total = sum(weights)
    delta = sum(w * d for w, (_, d) in zip(weights, entries)) / total
    return top + jnp.log(total), delta


NONE = -1e30


def unit_kernel(meta, mid, top, oth, topz, st, *refs):
    out_mid, out_top, mid_oth, top_far = refs[-4:]
    o1, o2 = head_offsets(meta, 0, meta[66])
    lap = lax.rem(o2, 16) == o1
    shift = lax.div(o2, 16)
    k1, v1 = (jnp.concatenate([mid[a], oth[a]], 0) for a in range(2))
    k2 = jnp.concatenate([topz[z, :64] for z in range(8)], 0)
    v2 = jnp.concatenate([topz[z, 64:] for z in range(8)], 0)
    q1, g1, q2, g2 = mid[2], mid[3], top[2], top[3]
    level0 = []
    for index in range(2):
        rows = jnp.concatenate([st[j, index : index + 1, :] for j in range(8)], 0).T
        level0.append(
            (
                jnp.concatenate([rows[:32, j : j + 1] for j in range(8)], 0),
                jnp.concatenate([rows[32:40, j : j + 1] for j in range(8)], 0),
            )
        )
    s1, s2 = dot_nt(q1, k1) * SCALE, dot_nt(q2, k2) * SCALE
    p1, p2 = dot_nt(g1, v1), dot_nt(g2, v2)
    lse1, d1 = softmax_stats(s1, p1)
    lse2, d2 = softmax_stats(s2, p2)
    up = (lane((64, 256)) == 4 * row((64, 256)) + shift) & lap
    down = (row((256, 64)) == 4 * lane((256, 64)) + shift) & lap
    one = jnp.ones((), F32)
    none = jnp.zeros((), F32)
    at_top = dot_nn(jnp.where(up, one, none).astype(BF16), encode_stats(lse1, d1, 256))
    at_mid = dot_nn(jnp.where(down, one, none).astype(BF16), encode_stats(lse2, d2, 64))
    lse1_top, d1_top = decode_stats(at_top)
    lse2_mid, d2_mid = decode_stats(at_mid)
    lse1_top = jnp.where(lap, lse1_top, NONE)
    has = (lax.rem(row((256, 1)), 4) == shift) & lap
    lse2_mid = jnp.where(has, lse2_mid, NONE)

    lse_m, delta_m = merge_stats([(level0[0][0], level0[1][0]), (lse1, d1), (lse2_mid, d2_mid)])
    lse_t, delta_t = merge_stats([(level0[0][1], level0[1][1]), (lse2, d2), (lse1_top, d1_top)])

    def back(score, dprob, lse, delta, q, k, v, g):
        prob = jnp.exp(score - lse)
        dscore = (prob * (dprob - delta)).astype(BF16)
        prob = prob.astype(BF16)
        return (
            dot_nn(prob, v).astype(BF16),
            (dot_nn(dscore, k) * SCALE).astype(BF16),
            dot_tn(dscore, q) * SCALE,
            dot_tn(prob, g),
        )

    oo, qq, kk, vv = back(s1, p1, lse_m, delta_m, q1, k1, v1, g1)
    out_mid[0] = oo
    out_mid[1] = qq
    out_mid[2] = kk[:256].astype(BF16)
    out_mid[3] = vv[:256].astype(BF16)
    out_mid[4] = encode_stats(lse_m, delta_m, 256)
    mid_oth[0] = kk[256:].astype(BF16)
    mid_oth[1] = vv[256:].astype(BF16)
    oo, qq, kk, vv = back(s2, p2, lse_t, delta_t, q2, k2, v2, g2)
    out_top[0] = oo
    out_top[1] = qq
    out_top[2] = encode_stats(lse_t, delta_t, 64)
    for z in range(8):
        top_far[z, :64] = kk[64 * z : 64 * z + 64].astype(BF16)
        top_far[z, 64:] = vv[64 * z : 64 * z + 64].astype(BF16)


def unit(meta, arrays, last):
    return pl.pallas_call(
        unit_kernel,
        out_shape=[
            jax.ShapeDtypeStruct((5, 256, 128), BF16),
            jax.ShapeDtypeStruct((3, 64, 128), BF16),
            jax.ShapeDtypeStruct((2, 256, 128), BF16),
            jax.ShapeDtypeStruct((8, 128, 128), BF16),
        ],
        in_specs=[SMEM] + [VMEM] * 5 + [ANY] * len(last),
        out_specs=[VMEM] * 4,
        compiler_params=params(),
        cost_estimate=COST,
        name="unit",
    )(meta, *arrays, *last)


def combine_kernel(out_mid, out_top, near, tops, *refs):
    back = refs[-1]
    top_kv = sum(tops[z].astype(F32) for z in range(8))
    mids = [out_mid[a].astype(F32) for a in range(5)]
    mids[2] = mids[2] + near[0].astype(F32)
    mids[3] = mids[3] + near[1].astype(F32)
    outs = [out_top[a].astype(F32) for a in range(3)]
    highs = [outs[0], outs[1], top_kv[:64], top_kv[64:]]
    for j in range(8):
        rows = [x[32 * j : 32 * j + 32] for x in mids[:4]]
        rows += [x[8 * j : 8 * j + 8] for x in highs]
        rows += [mids[4][32 * j : 32 * j + 32], outs[2][8 * j : 8 * j + 8]]
        back[j] = jnp.concatenate(rows, 0).astype(BF16)


def combine(arrays, last):
    return pl.pallas_call(
        combine_kernel,
        out_shape=jax.ShapeDtypeStruct((8, 200, 128), BF16),
        in_specs=[VMEM] * 4 + [ANY] * len(last),
        out_specs=VMEM,
        compiler_params=params(),
        cost_estimate=COST,
        name="combine",
    )(*arrays, *last)


def main_kernel(first, meta, *refs):
    kvs, qgs = refs[:4], refs[4:8]
    oqs, dk, dv = refs[-6:-2], refs[-2], refs[-1]
    for sub in range(2):
        main_head(first + 2 * pl.program_id(0) + sub, sub, meta, kvs, qgs, oqs, dk, dv)


def main_head(head, sub, meta, kvs, qgs, oqs, dk, dv):
    o1, o2 = head_offsets(meta, 0, head)
    cols = pl.ds(128 * sub, 128)
    key = jnp.concatenate([kv[:128, cols] for kv in kvs], 0)
    value = jnp.concatenate([kv[128:, cols] for kv in kvs], 0)
    query = jnp.concatenate([qg[:128, cols] for qg in qgs], 0)
    grad = jnp.concatenate([qg[128:, cols] for qg in qgs], 0)
    score = dot_nt(key, query) * (SCALE * LOG2E)
    weight = jnp.exp2(score - jnp.max(score, 0, keepdims=True))
    inverse = 1.0 / jnp.sum(weight, 0, keepdims=True)
    attended = dot_nn(value.T, weight.astype(BF16)) * inverse
    delta = jnp.sum(attended * grad.astype(F32).T, 0, keepdims=True)
    prob = weight * inverse
    dscore = (prob * (dot_nt(value, grad) - delta)).astype(BF16)
    attended = attended.T.astype(BF16)
    query_grad = (dot_nn(key.T, dscore) * SCALE).T.astype(BF16)
    for r in range(4):
        oqs[r][:128, cols] = attended[128 * r : 128 * r + 128]
        oqs[r][128:, cols] = query_grad[128 * r : 128 * r + 128]
    at = row((512, 128))
    active = (lax.rem(at, 16) == o1) | (lax.rem(at, 64) == o2)
    zero = jnp.zeros((), BF16)
    dk[sub] = dot_nn(dscore, jnp.where(active, zero, query)) * SCALE
    dv[sub] = dot_nn(prob.astype(BF16), jnp.where(active, zero, grad))


def pair_block(rows, first):
    return pl.BlockSpec((rows, 256), lambda h: (0, first // 2 + h))


def head_block(rows, first):
    return pl.BlockSpec((rows, 128), lambda h: (0, first + h))


def part_shapes(rows):
    return [jax.ShapeDtypeStruct((rows, 1024), BF16)] * 2 + [
        jax.ShapeDtypeStruct((rows, 512), BF16)
    ] * 2


def part_specs(rows, first):
    return [head_block(rows, first)] * 2 + [head_block(rows, 0)] * 2


def main(meta, kvs, qgs, first, held, last):
    before = [meta, *kvs, *qgs, *last]
    return pl.pallas_call(
        functools.partial(main_kernel, first),
        grid=(2,),
        out_shape=part_shapes(256) + [jax.ShapeDtypeStruct((4, 512, 128), F32)] * 2,
        in_specs=[SMEM]
        + [pair_block(256, first)] * 8
        + [ANY] * (len(last) + len(held)),
        out_specs=[pair_block(256, first)] * 2 + [pair_block(256, 0)] * 2
        + [pl.BlockSpec((2, 512, 128), lambda h: (h, 0, 0))] * 2,
        input_output_aliases={len(before) + i: i for i in range(len(held))},
        compiler_params=params(),
        cost_estimate=COST,
        name="main",
    )(*before, *held)


def late_kernel(first, meta, *refs):
    act, back, dk0, dv0 = refs[:4]
    kvs = refs[4:8]
    dkvs, oas, full = refs[-9:-5], refs[-5:-1], refs[-1]
    for sub in range(2):
        late_head(first + 2 * pl.program_id(0) + sub, sub, meta, act, back, dk0, dv0, kvs, dkvs, oas, full.at[sub])


def late_head(head, sub, meta, act, back, dk0, dv0, kvs, dkvs, oas, full):
    o1, o2 = head_offsets(meta, 0, head)
    at = pl.ds(128 * sub, 128)
    lap = lax.rem(o2, 16) == o1
    shift = lax.div(o2, 16)
    key = jnp.concatenate([kv[:128, at] for kv in kvs], 0)
    value = jnp.concatenate([kv[128:, at] for kv in kvs], 0)
    query, grad = act[2, :, at], act[3, :, at]
    ret = back[sub].astype(F32)
    lse, delta = decode_stats(ret[160:200])
    prob = jnp.exp(dot_nt(query, key) * SCALE - lse)
    dscore = (prob * (dot_nt(grad, value) - delta)).astype(BF16)
    prob = prob.astype(BF16)
    o_act, q_act = dot_nn(prob, value), dot_nn(dscore, key) * SCALE
    up = (lane((8, 32)) == 4 * row((8, 32)) + shift) & lap
    up = jnp.where(up, 1.0, 0.0).astype(BF16)
    o_mid = o_act[:32] + ret[0:32]
    q_mid = q_act[:32] + ret[32:64]
    o_top = o_act[32:] + ret[128:136] + dot_nn(up, ret[0:32].astype(BF16))
    q_top = q_act[32:] + ret[136:144] + dot_nn(up, ret[32:64].astype(BF16))
    for r in range(4):
        oas[r][:, at] = jnp.concatenate(
            [o_mid[8 * r : 8 * r + 8], q_mid[8 * r : 8 * r + 8], o_top, q_top], 0
        ).astype(BF16)
    twice = (row((40, 128)) >= 32) & lap
    for half, (start, weights, rows, mid_at, top_at, scale) in enumerate(
        ((dk0, dscore, query, 64, 144, SCALE), (dv0, prob, grad, 96, 152, 1.0))
    ):
        rows = jnp.where(twice, 0.0, rows.astype(F32)).astype(BF16)
        full[...] = start[sub] + dot_tn(weights, rows) * scale
        at_mid = pl.ds(o1, 32, stride=16)
        full[at_mid, :] = full[at_mid, :] + ret[mid_at : mid_at + 32]
        at_top = pl.ds(o2, 8, stride=64)
        full[at_top, :] = full[at_top, :] + ret[top_at : top_at + 8]
        for r in range(4):
            dkvs[r][half * 128 : half * 128 + 128, at] = full[128 * r : 128 * r + 128].astype(BF16)


def late(meta, act, back, dk0, dv0, kvs, first, held, last):
    before = [meta, act, back, dk0, dv0, *kvs, *last]
    places = (0, 1, 4, 5, 6, 7)[: len(held)]
    return pl.pallas_call(
        functools.partial(late_kernel, first),
        grid=(2,),
        out_shape=part_shapes(256) + [jax.ShapeDtypeStruct((32, 1024), BF16)] * 4,
        in_specs=[
            SMEM,
            pl.BlockSpec((4, 40, 256), lambda h: (0, 0, first // 2 + h)),
            pl.BlockSpec((2, 200, 128), lambda h: (first // 2 + h, 0, 0)),
            pl.BlockSpec((2, 512, 128), lambda h: (h, 0, 0)),
            pl.BlockSpec((2, 512, 128), lambda h: (h, 0, 0)),
        ]
        + [pair_block(256, first)] * 4
        + [ANY] * (len(last) + len(held)),
        out_specs=[pair_block(256, first)] * 2 + [pair_block(256, 0)] * 2 + [pair_block(32, first)] * 4,
        scratch_shapes=[pltpu.VMEM((2, 512, 128), F32)],
        input_output_aliases={len(before) + i: at for i, at in enumerate(places)},
        compiler_params=params(),
        cost_estimate=COST,
        name="late",
    )(*before, *held)


def piece(blocks, r, h):
    if r < 2:
        return blocks[r], 128 * h
    return blocks[2 * (h // 4) + r], h % 4 * 128


def finish_oq_kernel(meta, *refs):
    oqs, oas = refs[:6], refs[6:10]
    attended, query_grad, full = refs[-3:]
    group = meta[64]
    for r in range(4):
        for h in range(8):
            o1, o2 = head_offsets(meta, r, h)
            at = columns(group ^ r, h)
            source, near = piece(oqs, r, h)
            rows = oas[r][:, 128 * h : 128 * h + 128].astype(F32)
            for half, out in enumerate((attended, query_grad)):
                block = source[half * 128 : half * 128 + 128, near : near + 128]
                full[half] = block.astype(F32)
                full[half, pl.ds(o1, 8, stride=16), :] = rows[8 * half : 8 * half + 8]
                from_row = 16 + 8 * half + 2 * r
                full[half, pl.ds(o2, 2, stride=64), :] = rows[from_row : from_row + 2]
                out[:, at] = full[half].astype(BF16)


def finish_oq(meta, oqs, oas, last):
    return pl.pallas_call(
        finish_oq_kernel,
        out_shape=[jax.ShapeDtypeStruct((128, 4096), BF16)] * 2,
        in_specs=[SMEM] + [VMEM] * 10 + [ANY] * len(last),
        out_specs=[VMEM] * 2,
        scratch_shapes=[pltpu.VMEM((2, 128, 128), F32)],
        compiler_params=params(),
        cost_estimate=COST,
        name="finish_oq",
    )(meta, *oqs, *oas, *last)


def finish_kv_kernel(meta, *refs):
    dkvs, outs, held, sems = refs[:6], refs[6:8], refs[8], refs[9]
    group = meta[64]
    copies = []
    for half in range(2):
        for index, block in enumerate(dkvs):
            r = index if index < 4 else index - 2
            wide = 1024 if r < 2 else 512
            start = (group ^ r) * 1024 + (512 if index >= 4 else 0)
            at = pl.ds(pl.multiple_of(start, 128), wide)
            from_rows = block.at[pl.ds(half * 128, 128), :]
            copies.append(
                pltpu.make_async_copy(from_rows, held.at[half, :, at], sems.at[len(copies)])
            )
            copies[-1].start()
    stores = []
    for half in range(2):
        for copy in copies[6 * half : 6 * half + 6]:
            copy.wait()
        stores.append(pltpu.make_async_copy(held.at[half], outs[half], sems.at[12 + half]))
        stores[half].start()
    for copy in stores:
        copy.wait()


def finish_kv(meta, dkvs):
    return pl.pallas_call(
        finish_kv_kernel,
        out_shape=[jax.ShapeDtypeStruct((128, 4096), BF16)] * 2,
        in_specs=[SMEM] + [ANY] * 6,
        out_specs=[ANY] * 2,
        scratch_shapes=[pltpu.VMEM((2, 128, 4096), BF16), pltpu.SemaphoreType.DMA((14,))],
        compiler_params=params(),
        cost_estimate=COST,
        name="finish_kv",
    )(meta, *dkvs)


def local(query, key, value, out_grad, offsets):
    place = lax.axis_index("ctx")
    slot = lax.axis_index("head")
    xh, y = place // 4 % 2, place % 4
    group = slot ^ (2 * xh)
    routes = [None] + [rel_route(r) for r in (1, 2, 3)]
    units, levels = unit_groups(), z_groups()

    def go(block, r):
        return block if r == 0 else send(block, routes[r])

    def spread(blocks):
        return [go(block, r) for r, block in enumerate(blocks)]

    table = jnp.concatenate([block.reshape(16) for block in spread([offsets] * 4)])
    meta = jnp.concatenate([table, jnp.stack([group, 2 * xh, xh * 4 + y])])

    acts, kvs, qgs = open_blocks(meta, key, value, query, out_grad)
    acts = spread(acts)
    act, sent, passed = arrange(acts, kvs[1:])
    kvs = spread([kvs[0], *passed])
    qgs = spread(qgs)

    mid, top, far = fan(unit_exchange(sent, units))
    oth = send(mid[:2], ZL_ROUTE)
    topz = unit_exchange(far, levels)
    st = unit_exchange(stats(act, kvs, [topz]), units)
    out_mid, out_top, mid_oth, top_far = unit(meta, (mid, top, oth, topz, st), [qgs[2]])
    near = send(mid_oth, ZL_ROUTE)
    tops = unit_exchange(top_far, levels)
    first = main(meta, kvs, qgs, 0, [], [top_far])
    sums = combine((out_mid, out_top, near, tops), [first[4]])
    back = unit_exchange(sums, units)
    second = main(meta, kvs, qgs, 4, first[:2], [sums])
    oqs = [second[0], go(second[1], 1)]
    oqs += [go(first[2], 2), go(first[3], 3), go(second[2], 2), go(second[3], 3)]
    early = late(meta, act, back, first[4], first[5], kvs, 0, [], [second[4], oqs[2], oqs[3]])
    dkv2, dkv3 = send(early[2], routes[2]), send(early[3], routes[3])
    held = [early[0], early[1], *early[4:]]
    final = late(meta, act, back, second[4], second[5], kvs, 4, held, [oqs[4]])
    oas = spread(final[4:])
    dkvs = [final[0], go(final[1], 1), dkv2, dkv3, go(final[2], 2), go(final[3], 3)]
    attended, query_grad = finish_oq(meta, oqs, oas, [dkv2])
    key_grad, value_grad = finish_kv(meta, dkvs)
    return attended, query_grad, key_grad, value_grad


def solution(mesh):
    rows = P(AXES, None)
    return jax.shard_map(
        local,
        mesh=mesh,
        in_specs=(rows, rows, rows, rows, P(None, "head")),
        out_specs=(rows, rows, rows, rows),
        check_vma=False,
    )
```

```python
import functools

import jax
import jax.numpy as jnp
from jax import lax
from jax.experimental import pallas as pl
from jax.experimental.pallas import tpu as pltpu
from jax.sharding import PartitionSpec as P

AXES = ("ctx", "head")
SCALE = 128.0 ** -0.5
LOG2E = 1.4426950408889634
F32 = jnp.float32
BF16 = jnp.bfloat16
VMEM_LIMIT = 60 * 1024 * 1024


def decode(i):
    return i // 64, i // 32 % 2, i // 16 % 2, i // 4 % 4, i // 2 % 2, i % 2


def encode(s, zl, xh, y, xl, c):
    return ((((s * 2 + zl) * 2 + xh) * 4 + y) * 2 + xl) * 2 + c


def route(move):
    return [(i, encode(*move(*decode(i)))) for i in range(256)]


def rel_route(r):
    return route(lambda s, zl, xh, y, xl, c: (s, zl, xh, y, xl ^ (r >> 1), c ^ (r & 1)))


ZL_ROUTE = route(lambda s, zl, xh, y, xl, c: (s, zl ^ 1, xh, y, xl, c))


def unit_groups():
    groups = {}
    for i in range(256):
        s, zl, xh, y, xl, c = decode(i)
        groups.setdefault((s, zl, xl ^ xh, c), []).append(i)
    return list(groups.values())


def send(value, where):
    return lax.ppermute(value, AXES, where)


def z_groups():
    groups = {}
    for i in range(256):
        groups.setdefault(i % 32, []).append(i)
    return list(groups.values())


def unit_exchange(value, groups):
    flat = value.reshape(value.shape[0] * value.shape[1], 128)
    return lax.all_to_all(flat, AXES, 0, 0, tiled=True, axis_index_groups=groups).reshape(value.shape)


def dot_nt(a, b):
    return lax.dot_general(a, b, (((1,), (1,)), ((), ())), preferred_element_type=F32)


def dot_nn(a, b):
    return lax.dot_general(a, b, (((1,), (0,)), ((), ())), preferred_element_type=F32)


def dot_tn(a, b):
    return lax.dot_general(a, b, (((0,), (0,)), ((), ())), preferred_element_type=F32)


def params():
    return pltpu.CompilerParams(vmem_limit_bytes=VMEM_LIMIT)


COST = pl.CostEstimate(flops=0, bytes_accessed=1024, transcendentals=0)
SMEM = pl.BlockSpec(memory_space=pltpu.SMEM)
VMEM = pl.BlockSpec(memory_space=pltpu.VMEM)
ANY = pl.BlockSpec(memory_space=pl.ANY)


def columns(group, index):
    return pl.ds(pl.multiple_of(group * 1024 + index * 128, 128), 128)


def head_offsets(meta, r, h):
    at = (r ^ meta[65]) * 16 + h
    return meta[at], meta[at + 8]


def open_kernel(meta, key, value, query, grad, *refs):
    acts, blocks = refs[:4], refs[4:12]
    held, full, tops, sems, loads = refs[12:]
    group = meta[64]
    ready = []
    for a, ref in enumerate((key, value, query, grad)):
        ready.append(pltpu.make_async_copy(ref, held.at[a], loads.at[a]))
        ready[a].start()
    copies = []
    for a in range(4):
        ready[a].wait()
        for r in range(4):
            at = pl.ds(pl.multiple_of((group ^ r) * 1024, 128), 1024)
            to = blocks[a // 2 * 4 + r].at[pl.ds(a % 2 * 128, 128), :]
            copies.append(pltpu.make_async_copy(held.at[a, :, at], to, sems.at[4 * a + r]))
            copies[-1].start()
    for r in range(4):
        for h in range(8):
            o1, o2 = head_offsets(meta, r, h)
            at = columns(group ^ r, h)
            rows = []
            for a in range(4):
                full[a, :128] = held[a, :, at].astype(F32)
                rows.append(full[a, pl.ds(o1, 8, stride=16), :])
                tops[pl.ds(2 * a, 2), :] = full[a, pl.ds(o2, 2, stride=64), :]
            rows.append(tops[...])
            acts[r][:, h * 128 : h * 128 + 128] = jnp.concatenate(rows, 0).astype(BF16)
    for copy in copies:
        copy.wait()


def open_blocks(meta, key, value, query, grad):
    outs = pl.pallas_call(
        open_kernel,
        out_shape=[jax.ShapeDtypeStruct((40, 1024), BF16)] * 4
        + [jax.ShapeDtypeStruct((256, 1024), BF16)] * 8,
        in_specs=[SMEM] + [ANY] * 4,
        out_specs=[VMEM] * 4 + [ANY] * 8,
        scratch_shapes=[
            pltpu.VMEM((4, 128, 4096), BF16),
            pltpu.VMEM((4, 192, 128), F32),
            pltpu.VMEM((8, 128), F32),
            pltpu.SemaphoreType.DMA((16,)),
            pltpu.SemaphoreType.DMA((4,)),
        ],
        compiler_params=params(),
        cost_estimate=COST,
        name="open",
    )(meta, key, value, query, grad)
    return outs[:4], outs[4:8], outs[8:]


def arrange_kernel(a0, a1, a2, a3, *refs):
    act, out = refs[3:5]
    mid = [[] for _ in range(4)]
    top = [[] for _ in range(4)]
    for ref in (a0, a1, a2, a3):
        x = ref[...].astype(F32)
        for a in range(4):
            mid[a].append(x[8 * a : 8 * a + 8])
            top[a].append(x[32 + 2 * a : 34 + 2 * a])
    rows = []
    for a in range(4):
        rows.append(jnp.concatenate(mid[a] + [jnp.concatenate(top[a], 0)], 0))
        act[a] = rows[a].astype(BF16)
    whole = jnp.concatenate(rows, 0).astype(BF16)
    for h in range(8):
        out[h] = whole[:, 128 * h : 128 * h + 128]


def arrange(acts, blocks):
    outs = pl.pallas_call(
        arrange_kernel,
        out_shape=[
            jax.ShapeDtypeStruct((4, 40, 1024), BF16),
            jax.ShapeDtypeStruct((8, 160, 128), BF16),
        ]
        + [jax.ShapeDtypeStruct((256, 1024), BF16)] * 3,
        in_specs=[VMEM] * 4 + [ANY] * 3,
        out_specs=[VMEM] * 2 + [ANY] * 3,
        input_output_aliases={4: 2, 5: 3, 6: 4},
        compiler_params=params(),
        cost_estimate=COST,
        name="arrange",
    )(*acts, *blocks)
    return outs[0], outs[1], outs[2:]


def fan_kernel(got, mid, top, far):
    blocks = [got[j].astype(F32) for j in range(8)]
    tops = []
    for a in range(4):
        at = 40 * a
        mid[a] = jnp.concatenate([x[at : at + 32] for x in blocks], 0).astype(BF16)
        tops.append(jnp.concatenate([x[at + 32 : at + 40] for x in blocks], 0))
        top[a] = tops[a].astype(BF16)
    both_rows = jnp.concatenate(tops[:2], 0).astype(BF16)
    for z in range(8):
        far[z] = both_rows


def fan(got):
    return pl.pallas_call(
        fan_kernel,
        out_shape=[
            jax.ShapeDtypeStruct((4, 256, 128), BF16),
            jax.ShapeDtypeStruct((4, 64, 128), BF16),
            jax.ShapeDtypeStruct((8, 128, 128), BF16),
        ],
        in_specs=[VMEM],
        out_specs=[VMEM] * 3,
        compiler_params=params(),
        cost_estimate=COST,
        name="fan",
    )(got)


def lane(shape):
    return lax.broadcasted_iota(jnp.int32, shape, 1)


def row(shape):
    return lax.broadcasted_iota(jnp.int32, shape, 0)


def softmax_stats(score, dprob):
    top = jnp.max(score, -1, keepdims=True)
    weight = jnp.exp(score - top)
    total = jnp.sum(weight, -1, keepdims=True)
    delta = jnp.sum(weight * dprob, -1, keepdims=True) / total
    return top + jnp.log(total), delta


def stats_kernel(act, *refs):
    kvs, out = refs[:4], refs[-1]
    for h in range(8):
        at = pl.ds(128 * h, 128)
        key = jnp.concatenate([kv[:128, at] for kv in kvs], 0)
        value = jnp.concatenate([kv[128:, at] for kv in kvs], 0)
        score = dot_nt(key, act[2, :, at]) * SCALE
        top = jnp.max(score, 0, keepdims=True)
        weight = jnp.exp(score - top)
        total = jnp.sum(weight, 0, keepdims=True)
        dprob = dot_nt(value, act[3, :, at])
        out[h, 0:1, 0:40] = top + jnp.log(total)
        out[h, 1:2, 0:40] = jnp.sum(weight * dprob, 0, keepdims=True) / total


def stats(act, kvs, last):
    return pl.pallas_call(
        stats_kernel,
        out_shape=jax.ShapeDtypeStruct((8, 8, 128), F32),
        in_specs=[VMEM] * 5 + [ANY] * len(last),
        out_specs=VMEM,
        compiler_params=params(),
        cost_estimate=COST,
        name="stats",
    )(act, *kvs, *last)


def split_three(x):
    high = x.astype(BF16)
    rest = x - high.astype(F32)
    middle = rest.astype(BF16)
    low = (rest - middle.astype(F32)).astype(BF16)
    return high.astype(F32), middle.astype(F32), low.astype(F32)


def encode_stats(lse, delta, rows):
    at = lane((rows, 128))
    out = jnp.zeros((rows, 128), F32)
    for index, part in enumerate(split_three(lse) + split_three(delta)):
        out = jnp.where(at == index, part, out)
    return out.astype(BF16)


def decode_stats(x):
    at = lane(x.shape)
    lse = jnp.sum(jnp.where(at < 3, x, 0.0), -1, keepdims=True)
    delta = jnp.sum(jnp.where((at >= 3) & (at < 6), x, 0.0), -1, keepdims=True)
    return lse, delta


def merge_stats(entries):
    top = functools.reduce(jnp.maximum, [lse for lse, _ in entries])
    weights = [jnp.exp(lse - top) for lse, _ in entries]
    total = sum(weights)
    delta = sum(w * d for w, (_, d) in zip(weights, entries)) / total
    return top + jnp.log(total), delta


NONE = -1e30


def unit_kernel(meta, mid, top, oth, topz, st, *refs):
    out_mid, out_top, mid_oth, top_far = refs[-4:]
    o1, o2 = head_offsets(meta, 0, meta[66])
    lap = lax.rem(o2, 16) == o1
    shift = lax.div(o2, 16)
    k1, v1 = (jnp.concatenate([mid[a], oth[a]], 0) for a in range(2))
    k2 = jnp.concatenate([topz[z, :64] for z in range(8)], 0)
    v2 = jnp.concatenate([topz[z, 64:] for z in range(8)], 0)
    q1, g1, q2, g2 = mid[2], mid[3], top[2], top[3]
    level0 = []
    for index in range(2):
        rows = jnp.concatenate([st[j, index : index + 1, :] for j in range(8)], 0).T
        level0.append(
            (
                jnp.concatenate([rows[:32, j : j + 1] for j in range(8)], 0),
                jnp.concatenate([rows[32:40, j : j + 1] for j in range(8)], 0),
            )
        )
    s1, s2 = dot_nt(q1, k1) * SCALE, dot_nt(q2, k2) * SCALE
    p1, p2 = dot_nt(g1, v1), dot_nt(g2, v2)
    lse1, d1 = softmax_stats(s1, p1)
    lse2, d2 = softmax_stats(s2, p2)
    up = (lane((64, 256)) == 4 * row((64, 256)) + shift) & lap
    down = (row((256, 64)) == 4 * lane((256, 64)) + shift) & lap
    one = jnp.ones((), F32)
    none = jnp.zeros((), F32)
    at_top = dot_nn(jnp.where(up, one, none).astype(BF16), encode_stats(lse1, d1, 256))
    at_mid = dot_nn(jnp.where(down, one, none).astype(BF16), encode_stats(lse2, d2, 64))
    lse1_top, d1_top = decode_stats(at_top)
    lse2_mid, d2_mid = decode_stats(at_mid)
    lse1_top = jnp.where(lap, lse1_top, NONE)
    has = (lax.rem(row((256, 1)), 4) == shift) & lap
    lse2_mid = jnp.where(has, lse2_mid, NONE)

    lse_m, delta_m = merge_stats([(level0[0][0], level0[1][0]), (lse1, d1), (lse2_mid, d2_mid)])
    lse_t, delta_t = merge_stats([(level0[0][1], level0[1][1]), (lse2, d2), (lse1_top, d1_top)])

    def back(score, dprob, lse, delta, q, k, v, g):
        prob = jnp.exp(score - lse)
        dscore = (prob * (dprob - delta)).astype(BF16)
        prob = prob.astype(BF16)
        return (
            dot_nn(prob, v).astype(BF16),
            (dot_nn(dscore, k) * SCALE).astype(BF16),
            dot_tn(dscore, q) * SCALE,
            dot_tn(prob, g),
        )

    oo, qq, kk, vv = back(s1, p1, lse_m, delta_m, q1, k1, v1, g1)
    out_mid[0] = oo
    out_mid[1] = qq
    out_mid[2] = kk[:256].astype(BF16)
    out_mid[3] = vv[:256].astype(BF16)
    out_mid[4] = encode_stats(lse_m, delta_m, 256)
    mid_oth[0] = kk[256:].astype(BF16)
    mid_oth[1] = vv[256:].astype(BF16)
    oo, qq, kk, vv = back(s2, p2, lse_t, delta_t, q2, k2, v2, g2)
    out_top[0] = oo
    out_top[1] = qq
    out_top[2] = encode_stats(lse_t, delta_t, 64)
    for z in range(8):
        top_far[z, :64] = kk[64 * z : 64 * z + 64].astype(BF16)
        top_far[z, 64:] = vv[64 * z : 64 * z + 64].astype(BF16)


def unit(meta, arrays, last):
    return pl.pallas_call(
        unit_kernel,
        out_shape=[
            jax.ShapeDtypeStruct((5, 256, 128), BF16),
            jax.ShapeDtypeStruct((3, 64, 128), BF16),
            jax.ShapeDtypeStruct((2, 256, 128), BF16),
            jax.ShapeDtypeStruct((8, 128, 128), BF16),
        ],
        in_specs=[SMEM] + [VMEM] * 5 + [ANY] * len(last),
        out_specs=[VMEM] * 4,
        compiler_params=params(),
        cost_estimate=COST,
        name="unit",
    )(meta, *arrays, *last)


def combine_kernel(out_mid, out_top, near, tops, *refs):
    back = refs[-1]
    top_kv = sum(tops[z].astype(F32) for z in range(8))
    mids = [out_mid[a].astype(F32) for a in range(5)]
    mids[2] = mids[2] + near[0].astype(F32)
    mids[3] = mids[3] + near[1].astype(F32)
    outs = [out_top[a].astype(F32) for a in range(3)]
    highs = [outs[0], outs[1], top_kv[:64], top_kv[64:]]
    for j in range(8):
        rows = [x[32 * j : 32 * j + 32] for x in mids[:4]]
        rows += [x[8 * j : 8 * j + 8] for x in highs]
        rows += [mids[4][32 * j : 32 * j + 32], outs[2][8 * j : 8 * j + 8]]
        back[j] = jnp.concatenate(rows, 0).astype(BF16)


def combine(arrays, last):
    return pl.pallas_call(
        combine_kernel,
        out_shape=jax.ShapeDtypeStruct((8, 200, 128), BF16),
        in_specs=[VMEM] * 4 + [ANY] * len(last),
        out_specs=VMEM,
        compiler_params=params(),
        cost_estimate=COST,
        name="combine",
    )(*arrays, *last)


def main_kernel(first, meta, *refs):
    kvs, qgs = refs[:4], refs[4:8]
    oqs, dk, dv = refs[-6:-2], refs[-2], refs[-1]
    for sub in range(2):
        main_head(first + 2 * pl.program_id(0) + sub, sub, meta, kvs, qgs, oqs, dk, dv)


def main_head(head, sub, meta, kvs, qgs, oqs, dk, dv):
    o1, o2 = head_offsets(meta, 0, head)
    cols = pl.ds(128 * sub, 128)
    key = jnp.concatenate([kv[:128, cols] for kv in kvs], 0)
    value = jnp.concatenate([kv[128:, cols] for kv in kvs], 0)
    query = jnp.concatenate([qg[:128, cols] for qg in qgs], 0)
    grad = jnp.concatenate([qg[128:, cols] for qg in qgs], 0)
    score = dot_nt(key, query) * (SCALE * LOG2E)
    weight = jnp.exp2(score - jnp.max(score, 0, keepdims=True))
    inverse = 1.0 / jnp.sum(weight, 0, keepdims=True)
    attended = dot_nn(value.T, weight.astype(BF16)) * inverse
    delta = jnp.sum(attended * grad.astype(F32).T, 0, keepdims=True)
    prob = weight * inverse
    dscore = (prob * (dot_nt(value, grad) - delta)).astype(BF16)
    attended = attended.T.astype(BF16)
    query_grad = (dot_nn(key.T, dscore) * SCALE).T.astype(BF16)
    for r in range(4):
        oqs[r][:128, cols] = attended[128 * r : 128 * r + 128]
        oqs[r][128:, cols] = query_grad[128 * r : 128 * r + 128]
    at = row((512, 128))
    active = (lax.rem(at, 16) == o1) | (lax.rem(at, 64) == o2)
    zero = jnp.zeros((), BF16)
    dk[sub] = dot_nn(dscore, jnp.where(active, zero, query)) * SCALE
    dv[sub] = dot_nn(prob.astype(BF16), jnp.where(active, zero, grad))


def pair_block(rows, first):
    return pl.BlockSpec((rows, 256), lambda h: (0, first // 2 + h))


def head_block(rows, first):
    return pl.BlockSpec((rows, 128), lambda h: (0, first + h))


def part_shapes(rows):
    return [jax.ShapeDtypeStruct((rows, 1024), BF16)] * 2 + [
        jax.ShapeDtypeStruct((rows, 512), BF16)
    ] * 2


def part_specs(rows, first):
    return [head_block(rows, first)] * 2 + [head_block(rows, 0)] * 2


def main(meta, kvs, qgs, first, held, last):
    before = [meta, *kvs, *qgs, *last]
    return pl.pallas_call(
        functools.partial(main_kernel, first),
        grid=(2,),
        out_shape=part_shapes(256) + [jax.ShapeDtypeStruct((4, 512, 128), F32)] * 2,
        in_specs=[SMEM]
        + [pair_block(256, first)] * 8
        + [ANY] * (len(last) + len(held)),
        out_specs=[pair_block(256, first)] * 2 + [pair_block(256, 0)] * 2
        + [pl.BlockSpec((2, 512, 128), lambda h: (h, 0, 0))] * 2,
        input_output_aliases={len(before) + i: i for i in range(len(held))},
        compiler_params=params(),
        cost_estimate=COST,
        name="main",
    )(*before, *held)


def late_kernel(first, meta, *refs):
    act, back, dk0, dv0 = refs[:4]
    kvs = refs[4:8]
    dkvs, oas, full = refs[-9:-5], refs[-5:-1], refs[-1]
    for sub in range(2):
        late_head(first + 2 * pl.program_id(0) + sub, sub, meta, act, back, dk0, dv0, kvs, dkvs, oas, full.at[sub])


def late_head(head, sub, meta, act, back, dk0, dv0, kvs, dkvs, oas, full):
    o1, o2 = head_offsets(meta, 0, head)
    at = pl.ds(128 * sub, 128)
    lap = lax.rem(o2, 16) == o1
    shift = lax.div(o2, 16)
    key = jnp.concatenate([kv[:128, at] for kv in kvs], 0)
    value = jnp.concatenate([kv[128:, at] for kv in kvs], 0)
    query, grad = act[2, :, at], act[3, :, at]
    ret = back[sub].astype(F32)
    lse, delta = decode_stats(ret[160:200])
    prob = jnp.exp(dot_nt(query, key) * SCALE - lse)
    dscore = (prob * (dot_nt(grad, value) - delta)).astype(BF16)
    prob = prob.astype(BF16)
    o_act, q_act = dot_nn(prob, value), dot_nn(dscore, key) * SCALE
    up = (lane((8, 32)) == 4 * row((8, 32)) + shift) & lap
    up = jnp.where(up, 1.0, 0.0).astype(BF16)
    o_mid = o_act[:32] + ret[0:32]
    q_mid = q_act[:32] + ret[32:64]
    o_top = o_act[32:] + ret[128:136] + dot_nn(up, ret[0:32].astype(BF16))
    q_top = q_act[32:] + ret[136:144] + dot_nn(up, ret[32:64].astype(BF16))
    for r in range(4):
        oas[r][:, at] = jnp.concatenate(
            [o_mid[8 * r : 8 * r + 8], q_mid[8 * r : 8 * r + 8], o_top, q_top], 0
        ).astype(BF16)
    twice = (row((40, 128)) >= 32) & lap
    for half, (start, weights, rows, mid_at, top_at, scale) in enumerate(
        ((dk0, dscore, query, 64, 144, SCALE), (dv0, prob, grad, 96, 152, 1.0))
    ):
        rows = jnp.where(twice, 0.0, rows.astype(F32)).astype(BF16)
        full[:512] = start[sub] + dot_tn(weights, rows) * scale
        at_mid = pl.ds(o1, 32, stride=16)
        full[at_mid, :] = full[at_mid, :] + ret[mid_at : mid_at + 32]
        at_top = pl.ds(o2, 8, stride=64)
        full[at_top, :] = full[at_top, :] + ret[top_at : top_at + 8]
        for r in range(4):
            dkvs[r][half * 128 : half * 128 + 128, at] = full[128 * r : 128 * r + 128].astype(BF16)


def late(meta, act, back, dk0, dv0, kvs, first, held, last):
    before = [meta, act, back, dk0, dv0, *kvs, *last]
    places = (0, 1, 4, 5, 6, 7)[: len(held)]
    return pl.pallas_call(
        functools.partial(late_kernel, first),
        grid=(2,),
        out_shape=part_shapes(256) + [jax.ShapeDtypeStruct((32, 1024), BF16)] * 4,
        in_specs=[
            SMEM,
            pl.BlockSpec((4, 40, 256), lambda h: (0, 0, first // 2 + h)),
            pl.BlockSpec((2, 200, 128), lambda h: (first // 2 + h, 0, 0)),
            pl.BlockSpec((2, 512, 128), lambda h: (h, 0, 0)),
            pl.BlockSpec((2, 512, 128), lambda h: (h, 0, 0)),
        ]
        + [pair_block(256, first)] * 4
        + [ANY] * (len(last) + len(held)),
        out_specs=[pair_block(256, first)] * 2 + [pair_block(256, 0)] * 2 + [pair_block(32, first)] * 4,
        scratch_shapes=[pltpu.VMEM((2, 576, 128), F32)],
        input_output_aliases={len(before) + i: at for i, at in enumerate(places)},
        compiler_params=params(),
        cost_estimate=COST,
        name="late",
    )(*before, *held)


def piece(blocks, r, h):
    if r < 2:
        return blocks[r], 128 * h
    return blocks[2 * (h // 4) + r], h % 4 * 128


def finish_oq_kernel(meta, *refs):
    oqs, oas = refs[:6], refs[6:10]
    attended, query_grad, full = refs[-3:]
    group = meta[64]
    for r in range(4):
        for h in range(8):
            o1, o2 = head_offsets(meta, r, h)
            at = columns(group ^ r, h)
            source, near = piece(oqs, r, h)
            rows = oas[r][:, 128 * h : 128 * h + 128].astype(F32)
            for half, out in enumerate((attended, query_grad)):
                block = source[half * 128 : half * 128 + 128, near : near + 128]
                full[half, :128] = block.astype(F32)
                full[half, pl.ds(o1, 8, stride=16), :] = rows[8 * half : 8 * half + 8]
                from_row = 16 + 8 * half + 2 * r
                full[half, pl.ds(o2, 2, stride=64), :] = rows[from_row : from_row + 2]
                out[:, at] = full[half, :128].astype(BF16)


def finish_oq(meta, oqs, oas, last):
    return pl.pallas_call(
        finish_oq_kernel,
        out_shape=[jax.ShapeDtypeStruct((128, 4096), BF16)] * 2,
        in_specs=[SMEM] + [VMEM] * 10 + [ANY] * len(last),
        out_specs=[VMEM] * 2,
        scratch_shapes=[pltpu.VMEM((2, 192, 128), F32)],
        compiler_params=params(),
        cost_estimate=COST,
        name="finish_oq",
    )(meta, *oqs, *oas, *last)


def finish_kv_kernel(meta, *refs):
    dkvs, outs, held, sems = refs[:6], refs[6:8], refs[8], refs[9]
    group = meta[64]
    copies = []
    for half in range(2):
        for index, block in enumerate(dkvs):
            r = index if index < 4 else index - 2
            wide = 1024 if r < 2 else 512
            start = (group ^ r) * 1024 + (512 if index >= 4 else 0)
            at = pl.ds(pl.multiple_of(start, 128), wide)
            from_rows = block.at[pl.ds(half * 128, 128), :]
            copies.append(
                pltpu.make_async_copy(from_rows, held.at[half, :, at], sems.at[len(copies)])
            )
            copies[-1].start()
    stores = []
    for half in range(2):
        for copy in copies[6 * half : 6 * half + 6]:
            copy.wait()
        stores.append(pltpu.make_async_copy(held.at[half], outs[half], sems.at[12 + half]))
        stores[half].start()
    for copy in stores:
        copy.wait()


def finish_kv(meta, dkvs):
    return pl.pallas_call(
        finish_kv_kernel,
        out_shape=[jax.ShapeDtypeStruct((128, 4096), BF16)] * 2,
        in_specs=[SMEM] + [ANY] * 6,
        out_specs=[ANY] * 2,
        scratch_shapes=[pltpu.VMEM((2, 128, 4096), BF16), pltpu.SemaphoreType.DMA((14,))],
        compiler_params=params(),
        cost_estimate=COST,
        name="finish_kv",
    )(meta, *dkvs)


def local(query, key, value, out_grad, offsets):
    place = lax.axis_index("ctx")
    slot = lax.axis_index("head")
    xh, y = place // 4 % 2, place % 4
    group = slot ^ (2 * xh)
    routes = [None] + [rel_route(r) for r in (1, 2, 3)]
    units, levels = unit_groups(), z_groups()

    def go(block, r):
        return block if r == 0 else send(block, routes[r])

    def spread(blocks):
        return [go(block, r) for r, block in enumerate(blocks)]

    table = jnp.concatenate([block.reshape(16) for block in spread([offsets] * 4)])
    meta = jnp.concatenate([table, jnp.stack([group, 2 * xh, xh * 4 + y])])

    acts, kvs, qgs = open_blocks(meta, key, value, query, out_grad)
    acts = spread(acts)
    act, sent, passed = arrange(acts, kvs[1:])
    kvs = spread([kvs[0], *passed])
    qgs = spread(qgs)

    mid, top, far = fan(unit_exchange(sent, units))
    oth = send(mid[:2], ZL_ROUTE)
    topz = unit_exchange(far, levels)
    st = unit_exchange(stats(act, kvs, [topz]), units)
    out_mid, out_top, mid_oth, top_far = unit(meta, (mid, top, oth, topz, st), [qgs[2]])
    near = send(mid_oth, ZL_ROUTE)
    tops = unit_exchange(top_far, levels)
    first = main(meta, kvs, qgs, 0, [], [top_far])
    sums = combine((out_mid, out_top, near, tops), [first[4]])
    back = unit_exchange(sums, units)
    second = main(meta, kvs, qgs, 4, first[:2], [sums])
    oqs = [second[0], go(second[1], 1)]
    oqs += [go(first[2], 2), go(first[3], 3), go(second[2], 2), go(second[3], 3)]
    early = late(meta, act, back, first[4], first[5], kvs, 0, [], [second[4], oqs[2], oqs[3]])
    dkv2, dkv3 = send(early[2], routes[2]), send(early[3], routes[3])
    held = [early[0], early[1], *early[4:]]
    final = late(meta, act, back, second[4], second[5], kvs, 4, held, [oqs[4]])
    oas = spread(final[4:])
    dkvs = [final[0], go(final[1], 1), dkv2, dkv3, go(final[2], 2), go(final[3], 3)]
    attended, query_grad = finish_oq(meta, oqs, oas, [dkv2])
    key_grad, value_grad = finish_kv(meta, dkvs)
    return attended, query_grad, key_grad, value_grad


def solution(mesh):
    rows = P(AXES, None)
    return jax.shard_map(
        local,
        mesh=mesh,
        in_specs=(rows, rows, rows, rows, P(None, "head")),
        out_specs=(rows, rows, rows, rows),
        check_vma=False,
    )
```
